512 devices in a mesh: dp: 64 (over z, y), tensor: 8 (over x, core).
Axes of the slice: x: 4, y: 4, z: 16, core: 2. Of those that a mesh axis runs over, the one named last changes fastest.
Arguments:
- queries: bfloat16 [1024, 16, 24, 128], P('dp', None, 'tensor'), may hold values from -160 to 160
- new_kv: bfloat16 [1024, 2, 16, 8, 128], P('dp', None, None, 'tensor'), may hold values from -6 to 6
- kv_cache: bfloat16 [12288, 2, 16, 8, 128], P('dp', None, None, 'tensor'), may hold values from -6 to 6
- page_table: int32 [1024, 12], P('dp'), may hold values from 0 to 191, as said below
- lengths: int32 [1024], P('dp'), may hold values from 128 to 192, as said below
- out_proj: bfloat16 [3072, 2560], P('tensor'), may hold values from -0.109375 to 0.109375
- residual: bfloat16 [16384, 2560], P(('dp', 'tensor')), may hold values from -60 to 60
- norm_gain: bfloat16 [2560], replicated, may hold values from 0.099609375 to 1.8984375
- score_weight: bfloat16 [2560], replicated, may hold values from -0.125 to 0.125
- fork_parent: int32 [3072], P('dp'), may hold values from 0 to 1023, as said below
Outputs:
- hidden_out: bfloat16 [16384, 2560], P(('dp', 'tensor'))
- scores: float32 [1024], P(('dp', 'tensor'))
- child_pages: bfloat16 [3072, 8, 2, 16, 8, 128], P('dp', None, None, None, 'tensor')
The draws below stay inside these ranges and needn't reach their ends.
Inputs may be any that keep to these rules, and one draw needn't show every extreme that they name: `page_table`: the rows of one dp group use each of its 192 pages exactly once. `lengths`: some branch holds exactly 192 tokens. Among the child slots of one dp group, at most 2 have their parents in any one dp group, and that many in some pair; the parents that lie in one dp group (as fork_parent // 16) are at most 2 distinct branches over all child slots, and that many for some group.
All inputs are finite; a program needn't handle non-finite values.
Results may differ from the reference program's by a relative error of at most 0.008.
Values may be sent and summed in bfloat16 or wider, within the bound.
No kernel may reach another device: no remote copies, remote signals or barrier semaphores. Data moves between devices by JAX's collectives and lax.ppermute only.
A program may use at most 64 MiB of HBM per device.

```python
import math
import jax
import jax.numpy as jnp
from jax import lax

BR_DEV = 16
CH = 16
QH = 24
KVH = 8
HD = 128
DW = 2560
PAGE = 16
CTX = 192
PREFIX = 128
CHILD_DEV = 48
BRANCHES = 1024
CHILDREN = 3072
POOL_DEV = 192
POOL = 12288


def block_base(key):
    raw = jax.random.normal(key, (BRANCHES, 2, CH, KVH, HD), jnp.float32)
    return jnp.clip(raw, -6.0, 6.0)


def draw_new_kv(key, part):
    base = block_base(key)
    return base.astype(jnp.bfloat16)


def draw_queries(key, part):
    key = jax.random.fold_in(key, 5)
    entries = jnp.clip(jax.random.normal(key, (BRANCHES, CH, QH, HD), jnp.float32), -6.0, 6.0)
    return entries.astype(jnp.bfloat16)


def draw_residual(key, part):
    key = jax.random.fold_in(key, 9)
    parts_of = jax.random.split(key, 3)
    row_count = BRANCHES * CH
    row_scale = jnp.exp(0.5 * jax.random.uniform(parts_of[0], (row_count, 1), jnp.float32, 0.0, math.log(10.0)))
    col_scale = jnp.exp(0.5 * jax.random.uniform(parts_of[1], (1, DW), jnp.float32, 0.0, math.log(10.0)))
    noise = jnp.clip(jax.random.normal(parts_of[2], (row_count, DW), jnp.float32), -6.0, 6.0)
    return (0.4 * noise * row_scale * col_scale).astype(jnp.bfloat16)


def draw_lengths(key, part):
    key = jax.random.fold_in(key, 13)
    parts_of = jax.random.split(key, 2)
    drawn = jax.random.randint(parts_of[0], (BRANCHES,), PREFIX, CTX + 1)
    longest = jax.random.randint(parts_of[1], (), 0, BRANCHES)
    return jnp.where(jnp.arange(BRANCHES) == longest, CTX, drawn).astype(jnp.int32)


def draw_page_table(key, part):
    key = jax.random.fold_in(key, 17)
    groups = BRANCHES // BR_DEV
    pool_dev = BR_DEV * (CTX // PAGE)
    orders = jax.vmap(lambda sub: jax.random.permutation(sub, pool_dev))(jax.random.split(key, groups))
    return orders.reshape(BRANCHES, CTX // PAGE).astype(jnp.int32)


def draw_fork_parent(key, part):
    key = jax.random.fold_in(key, 19)
    parts_of = jax.random.split(key, 4)
    groups = CHILDREN // CHILD_DEV
    orders = jax.vmap(lambda sub: jax.random.permutation(sub, groups))(jax.random.split(parts_of[0], groups))
    pairs = jax.random.randint(parts_of[1], (groups, 1), 1, CHILD_DEV // 2 + 1)
    slots = jnp.arange(CHILD_DEV)[None, :]
    doubled = slots < 2 * pairs
    place = jnp.where(doubled, slots // 2, slots - pairs)
    sources = jnp.take_along_axis(orders, place, axis=1)
    picks = jax.vmap(lambda sub: jax.random.permutation(sub, BR_DEV)[:2])(jax.random.split(parts_of[2], groups))
    coins = jax.random.randint(parts_of[3], (groups, CHILD_DEV), 0, 2)
    which = jnp.where(doubled, slots % 2, coins)
    local_rows = picks[sources, which]
    return (sources * BR_DEV + local_rows).reshape(CHILDREN).astype(jnp.int32)


def steps_of(own_key, dims, shards, low, largest):
    level, own = 1.0, jax.random.fold_in(own_key, 6)
    for position, blocks in shards:
        steps = jnp.exp(jax.random.uniform(jax.random.fold_in(own, position), (blocks,), jnp.float32, low / len(shards), largest / len(shards)))
        level = level * jnp.repeat(steps, dims[position] // blocks).reshape([-1 if axis == position else 1 for axis in range(len(dims))])
    return level


def centred(stream_key, shape, width, limit, cuts=(), held_as=jnp.bfloat16):
    values = jax.random.normal(stream_key, shape, jnp.float32) * width
    if len(cuts) > 0:
        values = steps_of(stream_key, shape, cuts, -0.22, 0.18) * values
    return jnp.clip(values, min=-limit, max=limit).astype(held_as)


def setup_inputs(seed: int = 0) -> dict:
    key_of = jax.random.split(jax.random.key(seed), 11)
    return {
        "queries": draw_queries(jax.random.fold_in(key_of[10], 71), 0),
        "new_kv": draw_new_kv(jax.random.fold_in(key_of[10], 71), 0),
        "kv_cache": centred(key_of[2], (POOL, 2, PAGE, KVH, HD), 1.0, 6.0, ((0, 64), (3, 8))),
        "page_table": draw_page_table(jax.random.fold_in(key_of[10], 71), 0),
        "lengths": draw_lengths(jax.random.fold_in(key_of[10], 71), 0),
        "out_proj": centred(key_of[5], (QH * HD, DW), (QH * HD) ** -0.5, 0.109375, ((0, 8),)),
        "residual": draw_residual(jax.random.fold_in(key_of[10], 71), 0),
        "norm_gain": jnp.clip(1.0 + 0.18 * jax.random.normal(key_of[7], (DW,), jnp.float32), 0.099609375, 1.8984375).astype(jnp.bfloat16),
        "score_weight": centred(key_of[8], (DW,), DW ** -0.5, 0.125),
        "fork_parent": draw_fork_parent(jax.random.fold_in(key_of[10], 71), 0),
    }


neg_fill = -1e+30

def attend_group(inputs):
    queries, new_kv, pool_pages, table, lengths = inputs
    branch, steps_new, qheads, head_width = queries.shape
    kvheads = new_kv.shape[3]
    per_group = qheads // kvheads
    cache_pages = pool_pages[table]
    key_span = cache_pages.shape[1] * cache_pages.shape[3]
    cache_keys = cache_pages[:, :, 0].reshape(branch, key_span, kvheads, head_width).astype(jnp.float32)
    cache_values = cache_pages[:, :, 1].reshape(branch, key_span, kvheads, head_width).astype(jnp.float32)
    grouped = queries.reshape(branch, steps_new, kvheads, per_group, head_width).astype(jnp.float32)
    new_keys = new_kv[:, 0].astype(jnp.float32)
    new_values = new_kv[:, 1].astype(jnp.float32)
    score_scale = head_width ** (-0.5)
    old_scores = jnp.einsum('bckgd,bskd->bkgcs', grouped, cache_keys) * score_scale
    new_scores = jnp.einsum('bckgd,btkd->bkgct', grouped, new_keys) * score_scale
    old_mask = (jnp.arange(key_span)[None, :] < lengths[:, None])[:, None, None, None, :]
    new_mask = (jnp.arange(steps_new)[None, :] <= jnp.arange(steps_new)[:, None])[None, None, None]
    old_scores = jnp.where(old_mask, old_scores, neg_fill)
    new_scores = jnp.where(new_mask, new_scores, neg_fill)
    row_max = jnp.maximum(lax.optimization_barrier(jnp.max(old_scores, axis=-1, keepdims=True)), lax.optimization_barrier(jnp.max(new_scores, axis=-1, keepdims=True)))
    old_probs = jnp.where(old_mask, jnp.exp(old_scores - row_max), 0.0)
    new_probs = jnp.where(new_mask, jnp.exp(new_scores - row_max), 0.0)
    denom_sum = lax.optimization_barrier(jnp.sum(old_probs, axis=-1, keepdims=True)) + lax.optimization_barrier(jnp.sum(new_probs, axis=-1, keepdims=True))
    old_weights = (old_probs / denom_sum).astype(jnp.bfloat16)
    new_weights = (new_probs / denom_sum).astype(jnp.bfloat16)
    attended = jnp.einsum('bkgcs,bskd->bckgd', old_weights.astype(jnp.float32), cache_values)
    attended = attended + jnp.einsum('bkgct,btkd->bckgd', new_weights.astype(jnp.float32), new_values)
    return attended.astype(jnp.bfloat16)

def reference(queries, new_kv, kv_cache, page_table, lengths, out_proj, residual, norm_gain, score_weight, fork_parent):
    groups = BRANCHES // BR_DEV
    attended = lax.map(attend_group, (queries.reshape(groups, BR_DEV, CH, QH, HD), new_kv.reshape(groups, BR_DEV, 2, CH, KVH, HD), kv_cache.reshape(groups, POOL_DEV, 2, PAGE, KVH, HD), page_table.reshape(groups, BR_DEV, CTX // PAGE), lengths.reshape(groups, BR_DEV)))
    flat_rows = attended.reshape(BRANCHES * CH, QH * HD)
    updated = jnp.dot(flat_rows, out_proj, preferred_element_type=jnp.float32) + residual.astype(jnp.float32)
    hidden_out = updated.astype(jnp.bfloat16)
    block_ends = updated.reshape(BRANCHES, CH, DW)[:, CH - 1]
    normed = block_ends * lax.rsqrt(lax.optimization_barrier(jnp.mean(block_ends * block_ends, axis=-1, keepdims=True)) + 1e-06) * norm_gain.astype(jnp.float32)
    scores = jax.nn.sigmoid(lax.optimization_barrier(jnp.sum(normed * score_weight.astype(jnp.float32), axis=-1)))
    prefix_rows = page_table[fork_parent][:, :PREFIX // PAGE]
    owners = (fork_parent // BR_DEV)[:, None]
    child_pages = kv_cache[owners * POOL_DEV + prefix_rows]
    return (hidden_out, scores, child_pages)
```

```python
import jax
import jax.numpy as jnp
from jax import lax
from jax.sharding import PartitionSpec as P

BR_DEV = 16
CH = 16
PAGE = 16
PREFIX = 128


neg_fill = -1e30


def attend(queries, new_kv, kv_cache, page_table, lengths):
    branch, steps_new, qheads, head_width = queries.shape
    kvheads = new_kv.shape[3]
    per_group = qheads // kvheads
    cache_pages = kv_cache[page_table]
    key_span = cache_pages.shape[1] * cache_pages.shape[3]
    cache_keys = cache_pages[:, :, 0].reshape(branch, key_span, kvheads, head_width)
    cache_values = cache_pages[:, :, 1].reshape(branch, key_span, kvheads, head_width)
    grouped = queries.reshape(branch, steps_new, kvheads, per_group, head_width)
    score_scale = head_width ** (-0.5)
    old_scores = (
        jnp.einsum("bckgd,bskd->bkgcs", grouped, cache_keys, preferred_element_type=jnp.float32)
        * score_scale
    )
    new_scores = (
        jnp.einsum("bckgd,btkd->bkgct", grouped, new_kv[:, 0], preferred_element_type=jnp.float32)
        * score_scale
    )
    old_mask = (jnp.arange(key_span)[None, :] < lengths[:, None])[:, None, None, None, :]
    new_mask = (jnp.arange(steps_new)[None, :] <= jnp.arange(steps_new)[:, None])[None, None, None]
    old_scores = jnp.where(old_mask, old_scores, neg_fill)
    new_scores = jnp.where(new_mask, new_scores, neg_fill)
    row_max = jnp.maximum(
        jnp.max(old_scores, axis=-1, keepdims=True), jnp.max(new_scores, axis=-1, keepdims=True)
    )
    old_probs = jnp.where(old_mask, jnp.exp(old_scores - row_max), 0.0)
    new_probs = jnp.where(new_mask, jnp.exp(new_scores - row_max), 0.0)
    denom_sum = jnp.sum(old_probs, axis=-1, keepdims=True) + jnp.sum(
        new_probs, axis=-1, keepdims=True
    )
    old_weights = (old_probs / denom_sum).astype(jnp.bfloat16)
    new_weights = (new_probs / denom_sum).astype(jnp.bfloat16)
    attended = jnp.einsum(
        "bkgcs,bskd->bckgd", old_weights, cache_values, preferred_element_type=jnp.float32
    )
    attended = attended + jnp.einsum(
        "bkgct,btkd->bckgd", new_weights, new_kv[:, 1], preferred_element_type=jnp.float32
    )
    return attended.astype(jnp.bfloat16).reshape(branch * steps_new, qheads * head_width)


def parent_listing(fork_parent):
    groups = lax.axis_size("dp")
    slots = fork_parent.shape[0]
    row = jnp.pad(fork_parent, (0, 128 - slots))
    copies = jnp.broadcast_to(row[None, None, :], (groups, 1, 128))
    return lax.all_to_all(copies, "dp", split_axis=0, concat_axis=0, tiled=True)[:, 0, :slots]


def fork_pages(listing, fork_parent, kv_cache, page_table):
    groups = lax.axis_size("dp")
    me_index = lax.axis_index("dp")
    prefix_count = PREFIX // PAGE
    flat = listing.reshape(1, -1)
    asked = (flat // BR_DEV) == jnp.arange(groups)[:, None]
    lowest = jnp.min(jnp.where(asked, flat % BR_DEV, BR_DEV - 1), axis=1)
    highest = jnp.max(jnp.where(asked, flat % BR_DEV, 0), axis=1)
    mine = jnp.arange(groups) == me_index
    chosen = jnp.stack(
        [jnp.sum(jnp.where(mine, lowest, 0)), jnp.sum(jnp.where(mine, highest, 0))]
    )
    blocks = kv_cache[page_table[chosen][..., :prefix_count]]
    tile = blocks.shape
    gathered = lax.all_gather(blocks.reshape(-1, tile[-1]), "dp", axis=0, tiled=True)
    gathered = gathered.reshape((groups * 2,) + tile[1:])
    my_owner = fork_parent // BR_DEV
    hit = my_owner[:, None] == jnp.arange(groups)[None, :]
    first = jnp.sum(jnp.where(hit, lowest[None, :], 0), axis=1)
    second = (fork_parent % BR_DEV != first).astype(jnp.int32)
    return gathered[my_owner * 2 + second]


def local(
    queries,
    new_kv,
    kv_cache,
    page_table,
    lengths,
    out_proj,
    residual,
    norm_gain,
    score_weight,
    fork_parent,
):
    listing = parent_listing(fork_parent)
    attended = attend(queries, new_kv, kv_cache, page_table, lengths)
    rows_here = residual.shape[0]
    shards = lax.axis_size("tensor")
    partial = jnp.dot(attended, out_proj, preferred_element_type=jnp.float32).astype(jnp.bfloat16)
    terms = lax.all_to_all(
        partial.reshape(shards, rows_here, -1), "tensor", split_axis=0, concat_axis=0, tiled=True
    )
    updated = jnp.sum(terms.astype(jnp.float32), axis=0) + residual.astype(jnp.float32)
    hidden_out = updated.astype(jnp.bfloat16)
    block_ends = updated.reshape(rows_here // CH, CH, updated.shape[1])[:, CH - 1]
    normed = (
        block_ends
        * lax.rsqrt(jnp.mean(block_ends * block_ends, axis=-1, keepdims=True) + 1e-06)
        * norm_gain.astype(jnp.float32)
    )
    scores = jax.nn.sigmoid(jnp.sum(normed * score_weight.astype(jnp.float32), axis=-1))
    child_pages = fork_pages(listing, fork_parent, kv_cache, page_table)
    return (hidden_out, scores, child_pages)


def solution(mesh):
    in_specs = (
        P("dp", None, "tensor", None),
        P("dp", None, None, "tensor", None),
        P("dp", None, None, "tensor", None),
        P("dp", None),
        P("dp"),
        P("tensor", None),
        P(("dp", "tensor"), None),
        P(),
        P(),
        P("dp"),
    )
    out_specs = (
        P(("dp", "tensor"), None),
        P(("dp", "tensor")),
        P("dp", None, None, None, "tensor", None),
    )
    return jax.shard_map(local, mesh=mesh, in_specs=in_specs, out_specs=out_specs, check_vma=False)
```

```python
import jax
import jax.numpy as jnp
from jax import lax
from jax.experimental import pallas as pl
from jax.experimental.pallas import tpu as pltpu
from jax.sharding import PartitionSpec as P

BR_DEV = 16
CH = 16
PAGE = 16
PREFIX = 128
PAGES = PREFIX // PAGE
NZ, NY = 16, 4
LANES = 128


neg_fill = -1e30

def attend(queries, new_kv, kv_cache, page_table, lengths):
    branch, steps_new, qheads, head_width = queries.shape
    kvheads = new_kv.shape[3]
    per_group = qheads // kvheads
    cache_pages = kv_cache[page_table]
    key_span = cache_pages.shape[1] * cache_pages.shape[3]
    cache_keys = cache_pages[:, :, 0].reshape(branch, key_span, kvheads, head_width)
    cache_values = cache_pages[:, :, 1].reshape(branch, key_span, kvheads, head_width)
    grouped = queries.reshape(branch, steps_new, kvheads, per_group, head_width)
    score_scale = head_width ** (-0.5)
    old_scores = (
        jnp.einsum("bckgd,bskd->bkgcs", grouped, cache_keys, preferred_element_type=jnp.float32)
        * score_scale
    )
    new_scores = (
        jnp.einsum("bckgd,btkd->bkgct", grouped, new_kv[:, 0], preferred_element_type=jnp.float32)
        * score_scale
    )
    old_mask = (jnp.arange(key_span)[None, :] < lengths[:, None])[:, None, None, None, :]
    new_mask = (jnp.arange(steps_new)[None, :] <= jnp.arange(steps_new)[:, None])[None, None, None]
    old_scores = jnp.where(old_mask, old_scores, neg_fill)
    new_scores = jnp.where(new_mask, new_scores, neg_fill)
    row_max = jnp.maximum(
        jnp.max(old_scores, axis=-1, keepdims=True), jnp.max(new_scores, axis=-1, keepdims=True)
    )
    old_probs = jnp.where(old_mask, jnp.exp(old_scores - row_max), 0.0)
    new_probs = jnp.where(new_mask, jnp.exp(new_scores - row_max), 0.0)
    denom_sum = jnp.sum(old_probs, axis=-1, keepdims=True) + jnp.sum(
        new_probs, axis=-1, keepdims=True
    )
    old_weights = (old_probs / denom_sum).astype(jnp.bfloat16)
    new_weights = (new_probs / denom_sum).astype(jnp.bfloat16)
    attended = jnp.einsum(
        "bkgcs,bskd->bckgd", old_weights, cache_values, preferred_element_type=jnp.float32
    )
    attended = attended + jnp.einsum(
        "bkgct,btkd->bckgd", new_weights, new_kv[:, 1], preferred_element_type=jnp.float32
    )
    return attended.astype(jnp.bfloat16).reshape(branch * steps_new, qheads * head_width)


def parent_listing(fork_parent):
    groups = lax.axis_size("dp")
    slots = fork_parent.shape[0]
    row = jnp.pad(fork_parent, (0, LANES - slots), constant_values=-1)
    copies = jnp.broadcast_to(row[None, None, :], (groups, 1, LANES))
    return lax.all_to_all(copies, "dp", split_axis=0, concat_axis=0, tiled=True)[:, 0]


def shift_z(step):
    return [(z * NY + y, (z + step) % NZ * NY + y) for z in range(NZ) for y in range(NY)]


def shift_y(step):
    return [(z * NY + y, z * NY + (y + step) % NY) for z in range(NZ) for y in range(NY)]


def pick_kernel(me_ref, listing_ref, table_ref, cache_ref, low_ref, high_ref, sems):
    asked = listing_ref[...]
    mine = (asked >> 4) == me_ref[0]
    rows = asked & (BR_DEV - 1)
    lowest = jnp.min(jnp.where(mine, rows, BR_DEV - 1))
    highest = jnp.max(jnp.where(mine, rows, 0))
    copies = []
    for which, (row, out) in enumerate(((lowest, low_ref), (highest, high_ref))):
        for page in range(PAGES):
            copies.append(
                pltpu.make_async_copy(
                    cache_ref.at[table_ref[row, page]], out.at[page], sems.at[which, page]
                )
            )
    for copy in copies:
        copy.start()
    for copy in copies:
        copy.wait()


def pick_pages(me_index, listing, page_table, cache):
    block = jax.ShapeDtypeStruct((PAGES,) + cache.shape[1:], cache.dtype)
    return pl.pallas_call(
        pick_kernel,
        out_shape=(block, block),
        in_specs=[
            pl.BlockSpec(memory_space=pltpu.SMEM),
            pl.BlockSpec(memory_space=pltpu.VMEM),
            pl.BlockSpec(memory_space=pltpu.SMEM),
            pl.BlockSpec(memory_space=pl.ANY),
        ],
        out_specs=(pl.BlockSpec(memory_space=pl.ANY), pl.BlockSpec(memory_space=pl.ANY)),
        scratch_shapes=[pltpu.SemaphoreType.DMA((2, PAGES))],
    )(me_index.reshape(1), listing, page_table, cache)


def place_kernel(array_ref, index_ref, *refs):
    sources, out_ref, sems = refs[:-2], refs[-2], refs[-1]
    slots = out_ref.shape[0]

    @pl.loop(0, slots)
    def _(slot):
        for number, source in enumerate(sources):

            @pl.when(array_ref[slot] == number)
            def _():
                pltpu.make_async_copy(
                    source.at[index_ref[slot]], out_ref.at[slot], sems.at[slot]
                ).start()

    @pl.loop(0, slots)
    def _(slot):
        pltpu.make_async_copy(sources[0].at[0], out_ref.at[slot], sems.at[slot]).wait()


def place_children(array_of, index_of, sources):
    slots = array_of.shape[0]
    return pl.pallas_call(
        place_kernel,
        out_shape=jax.ShapeDtypeStruct((slots,) + sources[0].shape[1:], sources[0].dtype),
        in_specs=[pl.BlockSpec(memory_space=pltpu.SMEM)] * 2
        + [pl.BlockSpec(memory_space=pl.ANY)] * len(sources),
        out_specs=pl.BlockSpec(memory_space=pl.ANY),
        scratch_shapes=[pltpu.SemaphoreType.DMA((slots,))],
    )(array_of, index_of, *sources)


def spread(block, shifts):
    return [block] + [lax.ppermute(block, "dp", pairs) for pairs in shifts]


def fork_pages(listing, fork_parent, kv_cache, page_table):
    me_index = lax.axis_index("dp")
    me_z, me_y = me_index // NY, me_index % NY
    cache = kv_cache[:, :, :, 0]
    width = cache.shape[-1]
    low, high = pick_pages(me_index, listing, page_table, cache)
    rows = low.size // width
    both = jnp.concatenate([low.reshape(rows, width), high.reshape(rows, width)])

    far = spread(both, [shift_z(4), shift_z(8), shift_z(12)])
    low_far = jnp.concatenate([part[:rows] for part in far])
    high_far = jnp.concatenate([part[rows:] for part in far])
    near = [shift_z(1), shift_z(2), shift_z(-1)]
    across = [shift_y(1), shift_y(2), shift_y(3)]
    low_column = jnp.concatenate(spread(low_far, near))
    high_plane = jnp.concatenate(spread(high_far, across))
    low_column, high_plane = lax.optimization_barrier((low_column, high_plane))
    sources = spread(low_column, across) + spread(high_plane, near)
    sources = [part.reshape((NZ,) + low.shape) for part in sources]

    owner = fork_parent // BR_DEV
    asked = listing.reshape(1, -1)
    same = (asked // BR_DEV) == owner[:, None]
    first = jnp.min(jnp.where(same, asked % BR_DEV, BR_DEV - 1), axis=1)
    is_low = fork_parent % BR_DEV == first
    apart_z = (me_z - owner // NY) % NZ
    apart_y = (me_y - owner % NY) % NY
    near_z = apart_z % 4
    far_z = jnp.where(near_z == 3, apart_z + 1, apart_z) // 4 % 4
    array_of = jnp.where(is_low, apart_y, 4 + near_z)
    index_of = jnp.where(is_low, near_z, apart_y) * 4 + far_z
    placed = place_children(array_of.astype(jnp.int32), index_of.astype(jnp.int32), sources)
    return placed[:, :, :, :, None]


def local(
    queries,
    new_kv,
    kv_cache,
    page_table,
    lengths,
    out_proj,
    residual,
    norm_gain,
    score_weight,
    fork_parent,
):
    listing = parent_listing(fork_parent)
    attended = attend(queries, new_kv, kv_cache, page_table, lengths)
    rows_here = residual.shape[0]
    shards = lax.axis_size("tensor")
    partial = jnp.dot(attended, out_proj, preferred_element_type=jnp.float32).astype(jnp.bfloat16)
    terms = lax.all_to_all(
        partial.reshape(shards, rows_here, -1), "tensor", split_axis=0, concat_axis=0, tiled=True
    )
    updated = jnp.sum(terms.astype(jnp.float32), axis=0) + residual.astype(jnp.float32)
    hidden_out = updated.astype(jnp.bfloat16)
    block_ends = updated.reshape(rows_here // CH, CH, updated.shape[1])[:, CH - 1]
    normed = (
        block_ends
        * lax.rsqrt(jnp.mean(block_ends * block_ends, axis=-1, keepdims=True) + 1e-06)
        * norm_gain.astype(jnp.float32)
    )
    scores = jax.nn.sigmoid(jnp.sum(normed * score_weight.astype(jnp.float32), axis=-1))
    child_pages = fork_pages(listing, fork_parent, kv_cache, page_table)
    return (hidden_out, scores, child_pages)


def solution(mesh):
    in_specs = (
        P("dp", None, "tensor", None),
        P("dp", None, None, "tensor", None),
        P("dp", None, None, "tensor", None),
        P("dp", None),
        P("dp"),
        P("tensor", None),
        P(("dp", "tensor"), None),
        P(),
        P(),
        P("dp"),
    )
    out_specs = (
        P(("dp", "tensor"), None),
        P(("dp", "tensor")),
        P("dp", None, None, None, "tensor", None),
    )
    return jax.shard_map(local, mesh=mesh, in_specs=in_specs, out_specs=out_specs, check_vma=False)
```

```python
import functools

import jax
import jax.numpy as jnp
from jax import lax
from jax.experimental import pallas as pl
from jax.experimental.pallas import tpu as pltpu
from jax.sharding import PartitionSpec as P

BR_DEV = 16
CH = 16
PAGE = 16
PREFIX = 128
PAGES = PREFIX // PAGE
NZ, NY = 16, 4
NEAR = 4
LANES = 128


neg_fill = -1e30

def attend(queries, new_kv, kv_cache, page_table, lengths):
    branch, steps_new, qheads, head_width = queries.shape
    kvheads = new_kv.shape[3]
    per_group = qheads // kvheads
    cache_pages = kv_cache[page_table]
    key_span = cache_pages.shape[1] * cache_pages.shape[3]
    cache_keys = cache_pages[:, :, 0].reshape(branch, key_span, kvheads, head_width)
    cache_values = cache_pages[:, :, 1].reshape(branch, key_span, kvheads, head_width)
    grouped = queries.reshape(branch, steps_new, kvheads, per_group, head_width)
    score_scale = head_width ** (-0.5)
    old_scores = (
        jnp.einsum("bckgd,bskd->bkgcs", grouped, cache_keys, preferred_element_type=jnp.float32)
        * score_scale
    )
    new_scores = (
        jnp.einsum("bckgd,btkd->bkgct", grouped, new_kv[:, 0], preferred_element_type=jnp.float32)
        * score_scale
    )
    old_mask = (jnp.arange(key_span)[None, :] < lengths[:, None])[:, None, None, None, :]
    new_mask = (jnp.arange(steps_new)[None, :] <= jnp.arange(steps_new)[:, None])[None, None, None]
    old_scores = jnp.where(old_mask, old_scores, neg_fill)
    new_scores = jnp.where(new_mask, new_scores, neg_fill)
    row_max = jnp.maximum(
        jnp.max(old_scores, axis=-1, keepdims=True), jnp.max(new_scores, axis=-1, keepdims=True)
    )
    old_probs = jnp.where(old_mask, jnp.exp(old_scores - row_max), 0.0)
    new_probs = jnp.where(new_mask, jnp.exp(new_scores - row_max), 0.0)
    denom_sum = jnp.sum(old_probs, axis=-1, keepdims=True) + jnp.sum(
        new_probs, axis=-1, keepdims=True
    )
    old_weights = (old_probs / denom_sum).astype(jnp.bfloat16)
    new_weights = (new_probs / denom_sum).astype(jnp.bfloat16)
    attended = jnp.einsum(
        "bkgcs,bskd->bckgd", old_weights, cache_values, preferred_element_type=jnp.float32
    )
    attended = attended + jnp.einsum(
        "bkgct,btkd->bckgd", new_weights, new_kv[:, 1], preferred_element_type=jnp.float32
    )
    return attended.astype(jnp.bfloat16).reshape(branch * steps_new, qheads * head_width)


def parent_listing(fork_parent):
    groups = lax.axis_size("dp")
    slots = fork_parent.shape[0]
    row = jnp.pad(fork_parent, (0, LANES - slots), constant_values=-1)
    copies = jnp.broadcast_to(row[None, None, :], (groups, 1, LANES))
    return lax.all_to_all(copies, "dp", split_axis=0, concat_axis=0, tiled=True)[:, 0]


def shift_z(step):
    return [(z * NY + y, (z + step) % NZ * NY + y) for z in range(NZ) for y in range(NY)]


def shift_y(step):
    return [(z * NY + y, z * NY + (y + step) % NY) for z in range(NZ) for y in range(NY)]


def groups_far():
    return [[(near + NEAR * far) * NY + y for far in range(NZ // NEAR)] for near in range(NEAR) for y in range(NY)]


def groups_y():
    return [[z * NY + y for y in range(NY)] for z in range(NZ)]


def share(block, groups):
    copies = jnp.broadcast_to(block[None], (len(groups[0]),) + block.shape)
    return lax.all_to_all(
        copies, "dp", split_axis=0, concat_axis=0, tiled=True, axis_index_groups=groups
    )


def both_ways(block, shift):
    up = lax.ppermute(block, "dp", shift(1))
    down = lax.ppermute(block, "dp", shift(-1))
    return up, down


def forward(up, down, shift):
    half = up.shape[0] // 2
    up_two = lax.ppermute(up[:half], "dp", shift(1))
    down_two = lax.ppermute(down[half:], "dp", shift(-1))
    return up_two, down_two


def pick_kernel(me_ref, listing_ref, table_ref, cache_ref, out_ref, sems):
    asked = listing_ref[...]
    mine = (asked >> 4) == me_ref[0]
    rows = asked & (BR_DEV - 1)
    lowest = jnp.min(jnp.where(mine, rows, BR_DEV - 1))
    highest = jnp.max(jnp.where(mine, rows, 0))
    copies = []
    for which, row in enumerate((lowest, highest)):
        for page in range(PAGES):
            copies.append(
                pltpu.make_async_copy(
                    cache_ref.at[table_ref[row, page]], out_ref.at[which, page], sems.at[which, page]
                )
            )
    for copy in copies:
        copy.start()
    for copy in copies:
        copy.wait()


def pick_pages(me_index, listing, page_table, cache):
    return pl.pallas_call(
        pick_kernel,
        out_shape=jax.ShapeDtypeStruct((2, PAGES) + cache.shape[1:], cache.dtype),
        in_specs=[
            pl.BlockSpec(memory_space=pltpu.SMEM),
            pl.BlockSpec(memory_space=pltpu.VMEM),
            pl.BlockSpec(memory_space=pltpu.SMEM),
            pl.BlockSpec(memory_space=pl.ANY),
        ],
        out_specs=pl.BlockSpec(memory_space=pltpu.VMEM),
        scratch_shapes=[pltpu.SemaphoreType.DMA((2, PAGES))],
    )(me_index.reshape(1), listing, page_table, cache)


def place_kernel(count, aliased, where_ref, *refs):
    sources = refs[:count]
    out_ref, held, load_sems, sems = refs[count + aliased :]
    slots = out_ref.shape[0]
    loads, base = [], 0
    for number, source in enumerate(sources):
        size = source.shape[0]
        loads.append(
            pltpu.make_async_copy(source, held.at[pl.ds(base, size)], load_sems.at[number])
        )
        base += size
    for load in loads:
        load.start()
    for load in loads:
        load.wait()

    @pl.loop(0, slots)
    def _(slot):
        where = where_ref[slot]

        @pl.when(where >= 0)
        def _():
            pltpu.make_async_copy(held.at[where], out_ref.at[slot], sems.at[slot]).start()

    @pl.loop(0, slots)
    def _(slot):
        @pl.when(where_ref[slot] >= 0)
        def _():
            pltpu.make_async_copy(held.at[0], out_ref.at[slot], sems.at[slot]).wait()


def place_children(where, sources, earlier=None):
    slots = where.shape[0]
    count = len(sources)
    blocks = sum(source.shape[0] for source in sources)
    tile = sources[0].shape[1:]
    given = [where] + list(sources) + ([] if earlier is None else [earlier])
    return pl.pallas_call(
        functools.partial(place_kernel, count, len(given) - 1 - count),
        out_shape=jax.ShapeDtypeStruct((slots,) + tile, sources[0].dtype),
        in_specs=[pl.BlockSpec(memory_space=pltpu.SMEM)]
        + [pl.BlockSpec(memory_space=pl.ANY)] * (len(given) - 1),
        out_specs=pl.BlockSpec(memory_space=pl.ANY),
        scratch_shapes=[
            pltpu.VMEM((blocks,) + tile, sources[0].dtype),
            pltpu.SemaphoreType.DMA((count,)),
            pltpu.SemaphoreType.DMA((slots,)),
        ],
        input_output_aliases={} if earlier is None else {len(given) - 1: 0},
        compiler_params=pltpu.CompilerParams(vmem_limit_bytes=24 * 2**20),
    )(*given)


def child_places(listing, fork_parent, me_z, me_y):
    owner = fork_parent // BR_DEV
    asked = listing.reshape(1, -1)
    same = (asked // BR_DEV) == owner[:, None]
    first = jnp.min(jnp.where(same, asked % BR_DEV, BR_DEV - 1), axis=1)
    is_low = fork_parent % BR_DEV == first
    owner_z, owner_y = owner // NY, owner % NY
    far = owner_z // NEAR
    near = (me_z - owner_z) % NEAR
    apart = (me_y - owner_y) % NY
    step = jnp.where(is_low, apart, near)
    inner = jnp.where(is_low, near, owner_y) * (NZ // NEAR) + far
    place = jnp.where(step == 0, 0, jnp.where(step == 1, NZ, 2 * NZ)) + inner
    early = jnp.where(step == 2, -1, place + jnp.where(is_low, 0, 3 * NZ))
    late = jnp.where(step == 2, inner + jnp.where(is_low, 0, NZ), -1)
    return early.astype(jnp.int32), late.astype(jnp.int32)


def gather_near(listing, kv_cache, page_table):
    me_index = lax.axis_index("dp")
    cache = kv_cache[:, :, :, 0]
    width = cache.shape[-1]
    picked = pick_pages(me_index, listing, page_table, cache)
    rows = picked[0].size // width

    far = share(picked.reshape(2 * rows, width), groups_far())
    low_far = far[:, :rows].reshape(-1, width)
    high_far = far[:, rows:].reshape(-1, width)
    high_plane = share(high_far, groups_y()).reshape(-1, width)
    low_column = jnp.concatenate(
        [low_far] + [lax.ppermute(low_far, "dp", shift_z(step)) for step in (1, 2, -1)]
    )
    return low_column, high_plane, picked.shape[1:]


def fork_pages(listing, fork_parent, low_column, high_plane, tile):
    me_index = lax.axis_index("dp")
    me_z, me_y = me_index // NY, me_index % NY
    early, late = child_places(listing, fork_parent, me_z, me_y)
    low_up, low_down = both_ways(low_column, shift_y)
    high_up, high_down = both_ways(high_plane, shift_z)
    low_two = forward(low_up, low_down, shift_y)
    high_two = forward(high_up, high_down, shift_z)
    first = (low_column, low_up, low_down, high_plane, high_up, high_down)
    placed = place_children(early, [part.reshape((-1,) + tile) for part in first])
    placed = place_children(
        late, [part.reshape((-1,) + tile) for part in low_two + high_two], placed
    )
    return placed[:, :, :, :, None]


def local(
    queries,
    new_kv,
    kv_cache,
    page_table,
    lengths,
    out_proj,
    residual,
    norm_gain,
    score_weight,
    fork_parent,
):
    listing = parent_listing(fork_parent)
    attended = attend(queries, new_kv, kv_cache, page_table, lengths)
    rows_here = residual.shape[0]
    shards = lax.axis_size("tensor")
    partial = jnp.dot(attended, out_proj, preferred_element_type=jnp.float32).astype(jnp.bfloat16)
    low_column, high_plane, tile = gather_near(listing, kv_cache, page_table)
    low_column, high_plane, partial = lax.optimization_barrier((low_column, high_plane, partial))
    terms = lax.all_to_all(
        partial.reshape(shards, rows_here, -1), "tensor", split_axis=0, concat_axis=0, tiled=True
    )
    updated = jnp.sum(terms.astype(jnp.float32), axis=0) + residual.astype(jnp.float32)
    hidden_out = updated.astype(jnp.bfloat16)
    block_ends = updated.reshape(rows_here // CH, CH, updated.shape[1])[:, CH - 1]
    normed = (
        block_ends
        * lax.rsqrt(jnp.mean(block_ends * block_ends, axis=-1, keepdims=True) + 1e-06)
        * norm_gain.astype(jnp.float32)
    )
    scores = jax.nn.sigmoid(jnp.sum(normed * score_weight.astype(jnp.float32), axis=-1))
    child_pages = fork_pages(listing, fork_parent, low_column, high_plane, tile)
    return (hidden_out, scores, child_pages)


def solution(mesh):
    in_specs = (
        P("dp", None, "tensor", None),
        P("dp", None, None, "tensor", None),
        P("dp", None, None, "tensor", None),
        P("dp", None),
        P("dp"),
        P("tensor", None),
        P(("dp", "tensor"), None),
        P(),
        P(),
        P("dp"),
    )
    out_specs = (
        P(("dp", "tensor"), None),
        P(("dp", "tensor")),
        P("dp", None, None, None, "tensor", None),
    )
    return jax.shard_map(local, mesh=mesh, in_specs=in_specs, out_specs=out_specs, check_vma=False)
```

```python
import functools

import jax
import jax.numpy as jnp
from jax import lax
from jax.experimental import pallas as pl
from jax.experimental.pallas import tpu as pltpu
from jax.sharding import PartitionSpec as P

BR_DEV = 16
CH = 16
PAGE = 16
PREFIX = 128
PAGES = PREFIX // PAGE
NZ, NY = 16, 4
NEAR = 4
FRONT = 6
LANES = 128


neg_fill = -1e30

def attend(queries, new_kv, kv_cache, page_table, lengths):
    branch, steps_new, qheads, head_width = queries.shape
    kvheads = new_kv.shape[3]
    per_group = qheads // kvheads
    cache_pages = kv_cache[page_table]
    key_span = cache_pages.shape[1] * cache_pages.shape[3]
    cache_keys = cache_pages[:, :, 0].reshape(branch, key_span, kvheads, head_width)
    cache_values = cache_pages[:, :, 1].reshape(branch, key_span, kvheads, head_width)
    grouped = queries.reshape(branch, steps_new, kvheads, per_group, head_width)
    score_scale = head_width ** (-0.5)
    old_scores = (
        jnp.einsum("bckgd,bskd->bkgcs", grouped, cache_keys, preferred_element_type=jnp.float32)
        * score_scale
    )
    new_scores = (
        jnp.einsum("bckgd,btkd->bkgct", grouped, new_kv[:, 0], preferred_element_type=jnp.float32)
        * score_scale
    )
    old_mask = (jnp.arange(key_span)[None, :] < lengths[:, None])[:, None, None, None, :]
    new_mask = (jnp.arange(steps_new)[None, :] <= jnp.arange(steps_new)[:, None])[None, None, None]
    old_scores = jnp.where(old_mask, old_scores, neg_fill)
    new_scores = jnp.where(new_mask, new_scores, neg_fill)
    row_max = jnp.maximum(
        jnp.max(old_scores, axis=-1, keepdims=True), jnp.max(new_scores, axis=-1, keepdims=True)
    )
    old_probs = jnp.where(old_mask, jnp.exp(old_scores - row_max), 0.0)
    new_probs = jnp.where(new_mask, jnp.exp(new_scores - row_max), 0.0)
    denom_sum = jnp.sum(old_probs, axis=-1, keepdims=True) + jnp.sum(
        new_probs, axis=-1, keepdims=True
    )
    old_weights = (old_probs / denom_sum).astype(jnp.bfloat16)
    new_weights = (new_probs / denom_sum).astype(jnp.bfloat16)
    attended = jnp.einsum(
        "bkgcs,bskd->bckgd", old_weights, cache_values, preferred_element_type=jnp.float32
    )
    attended = attended + jnp.einsum(
        "bkgct,btkd->bckgd", new_weights, new_kv[:, 1], preferred_element_type=jnp.float32
    )
    return attended.astype(jnp.bfloat16).reshape(branch * steps_new, qheads * head_width)


def parent_listing(fork_parent):
    groups = lax.axis_size("dp")
    slots = fork_parent.shape[0]
    row = jnp.pad(fork_parent, (0, LANES - slots), constant_values=-1)
    copies = jnp.broadcast_to(row[None, None, :], (groups, 1, LANES))
    return lax.all_to_all(copies, "dp", split_axis=0, concat_axis=0, tiled=True)[:, 0]


def shift_z(step):
    return [(z * NY + y, (z + step) % NZ * NY + y) for z in range(NZ) for y in range(NY)]


def groups_far():
    return [[(near + NEAR * far) * NY + y for far in range(NZ // NEAR)] for near in range(NEAR) for y in range(NY)]


def groups_z():
    return [[z * NY + y for z in range(NZ)] for y in range(NY)]


def groups_y():
    return [[z * NY + y for y in range(NY)] for z in range(NZ)]


def share(block, groups):
    copies = jnp.broadcast_to(block[None], (len(groups[0]),) + block.shape)
    return lax.all_to_all(
        copies, "dp", split_axis=0, concat_axis=0, tiled=True, axis_index_groups=groups
    )


def pick_kernel(me_ref, listing_ref, table_ref, cache_ref, front_ref, back_ref, sems):
    asked = listing_ref[...]
    mine = (asked >> 4) == me_ref[0]
    rows = asked & (BR_DEV - 1)
    lowest = jnp.min(jnp.where(mine, rows, BR_DEV - 1))
    highest = jnp.max(jnp.where(mine, rows, 0))
    copies = []
    for which, row in enumerate((lowest, highest)):
        for page in range(PAGES):
            target = front_ref.at[which, page] if page < FRONT else back_ref.at[which, page - FRONT]
            copies.append(
                pltpu.make_async_copy(
                    cache_ref.at[table_ref[row, page]], target, sems.at[which, page]
                )
            )
    for copy in copies:
        copy.start()
    for copy in copies:
        copy.wait()


def pick_pages(me_index, listing, page_table, cache):
    return pl.pallas_call(
        pick_kernel,
        out_shape=tuple(
            jax.ShapeDtypeStruct((2, pages) + cache.shape[1:], cache.dtype)
            for pages in (FRONT, PAGES - FRONT)
        ),
        in_specs=[
            pl.BlockSpec(memory_space=pltpu.SMEM),
            pl.BlockSpec(memory_space=pltpu.VMEM),
            pl.BlockSpec(memory_space=pltpu.SMEM),
            pl.BlockSpec(memory_space=pl.ANY),
        ],
        out_specs=(pl.BlockSpec(memory_space=pltpu.VMEM),) * 2,
        scratch_shapes=[pltpu.SemaphoreType.DMA((2, PAGES))],
    )(me_index.reshape(1), listing, page_table, cache)


def place_kernel(first_page, aliased, where_ref, source_ref, *refs):
    out_ref, sems = refs[aliased:]
    slots = out_ref.shape[0]
    pages = source_ref.shape[1]

    def store(slot):
        return pltpu.make_async_copy(
            source_ref.at[where_ref[slot]], out_ref.at[slot, pl.ds(first_page, pages)], sems.at[slot]
        )

    @pl.loop(0, slots)
    def _(slot):
        store(slot).start()

    @pl.loop(0, slots)
    def _(slot):
        store(slot).wait()


def place_children(where, source, first_page, earlier=None):
    slots = where.shape[0]
    given = [where, source] + ([] if earlier is None else [earlier])
    return pl.pallas_call(
        functools.partial(place_kernel, first_page, len(given) - 2),
        out_shape=jax.ShapeDtypeStruct((slots, PAGES) + source.shape[2:], source.dtype),
        in_specs=[
            pl.BlockSpec(memory_space=pltpu.SMEM),
            pl.BlockSpec(memory_space=pltpu.VMEM),
        ]
        + [pl.BlockSpec(memory_space=pl.ANY)] * (len(given) - 2),
        out_specs=pl.BlockSpec(memory_space=pl.ANY),
        scratch_shapes=[pltpu.SemaphoreType.DMA((slots,))],
        input_output_aliases={} if earlier is None else {2: 0},
        compiler_params=pltpu.CompilerParams(vmem_limit_bytes=24 * 2**20),
    )(*given)


def child_places(listing, fork_parent, me_index):
    owner = fork_parent // BR_DEV
    asked = listing.reshape(1, -1)
    same = (asked // BR_DEV) == owner[:, None]
    first = jnp.min(jnp.where(same, asked % BR_DEV, BR_DEV - 1), axis=1)
    which = (fork_parent % BR_DEV != first).astype(jnp.int32)
    owner_z, owner_y = owner // NY, owner % NY
    near = (me_index // NY - owner_z) % NEAR
    front = owner * 2 + which
    back = ((owner_y * NEAR + near) * (NZ // NEAR) + owner_z // NEAR) * 2 + which
    return front, back


def gather_parents(listing, kv_cache, page_table):
    cache = kv_cache[:, :, :, 0]
    width = cache.shape[-1]
    front, back = pick_pages(lax.axis_index("dp"), listing, page_table, cache)
    plane = share(front.reshape(-1, width), groups_y()).reshape(-1, width)
    fronts = lax.all_gather(plane, "dp", axis=0, tiled=True, axis_index_groups=groups_z())
    far = share(back.reshape(-1, width), groups_far()).reshape(-1, width)
    column = jnp.concatenate(
        [far] + [lax.ppermute(far, "dp", shift_z(step)) for step in (1, 2, -1)]
    )
    backs = share(column, groups_y()).reshape(-1, width)
    return fronts.reshape((-1,) + front.shape[1:]), backs.reshape((-1,) + back.shape[1:])


def local(
    queries,
    new_kv,
    kv_cache,
    page_table,
    lengths,
    out_proj,
    residual,
    norm_gain,
    score_weight,
    fork_parent,
):
    listing = parent_listing(fork_parent)
    attended = attend(queries, new_kv, kv_cache, page_table, lengths)
    rows_here = residual.shape[0]
    shards = lax.axis_size("tensor")
    partial = jnp.dot(attended, out_proj, preferred_element_type=jnp.float32).astype(jnp.bfloat16)
    fronts, backs = gather_parents(listing, kv_cache, page_table)
    backs, partial = lax.optimization_barrier((backs, partial))
    terms = lax.all_to_all(
        partial.reshape(shards, rows_here, -1), "tensor", split_axis=0, concat_axis=0, tiled=True
    )
    updated = jnp.sum(terms.astype(jnp.float32), axis=0) + residual.astype(jnp.float32)
    hidden_out = updated.astype(jnp.bfloat16)
    block_ends = updated.reshape(rows_here // CH, CH, updated.shape[1])[:, CH - 1]
    normed = (
        block_ends
        * lax.rsqrt(jnp.mean(block_ends * block_ends, axis=-1, keepdims=True) + 1e-06)
        * norm_gain.astype(jnp.float32)
    )
    scores = jax.nn.sigmoid(jnp.sum(normed * score_weight.astype(jnp.float32), axis=-1))
    front_at, back_at = child_places(listing, fork_parent, lax.axis_index("dp"))
    child_pages = place_children(back_at, backs, FRONT)
    child_pages = place_children(front_at, fronts, 0, child_pages)[:, :, :, :, None]
    return (hidden_out, scores, child_pages)


def solution(mesh):
    in_specs = (
        P("dp", None, "tensor", None),
        P("dp", None, None, "tensor", None),
        P("dp", None, None, "tensor", None),
        P("dp", None),
        P("dp"),
        P("tensor", None),
        P(("dp", "tensor"), None),
        P(),
        P(),
        P("dp"),
    )
    out_specs = (
        P(("dp", "tensor"), None),
        P(("dp", "tensor")),
        P("dp", None, None, None, "tensor", None),
    )
    return jax.shard_map(local, mesh=mesh, in_specs=in_specs, out_specs=out_specs, check_vma=False)
```

```python
import functools

import jax
import jax.numpy as jnp
from jax import lax
from jax.experimental import pallas as pl
from jax.experimental.pallas import tpu as pltpu
from jax.sharding import PartitionSpec as P

BR_DEV = 16
CH = 16
PAGE = 16
PREFIX = 128
PAGES = PREFIX // PAGE
NZ, NY = 16, 4
NEAR = 4
LANES = 128


neg_fill = -1e30

def attend(queries, new_kv, kv_cache, page_table, lengths):
    branch, steps_new, qheads, head_width = queries.shape
    kvheads = new_kv.shape[3]
    per_group = qheads // kvheads
    cache_pages = kv_cache[page_table]
    key_span = cache_pages.shape[1] * cache_pages.shape[3]
    cache_keys = cache_pages[:, :, 0].reshape(branch, key_span, kvheads, head_width)
    cache_values = cache_pages[:, :, 1].reshape(branch, key_span, kvheads, head_width)
    grouped = queries.reshape(branch, steps_new, kvheads, per_group, head_width)
    score_scale = head_width ** (-0.5)
    old_scores = (
        jnp.einsum("bckgd,bskd->bkgcs", grouped, cache_keys, preferred_element_type=jnp.float32)
        * score_scale
    )
    new_scores = (
        jnp.einsum("bckgd,btkd->bkgct", grouped, new_kv[:, 0], preferred_element_type=jnp.float32)
        * score_scale
    )
    old_mask = (jnp.arange(key_span)[None, :] < lengths[:, None])[:, None, None, None, :]
    new_mask = (jnp.arange(steps_new)[None, :] <= jnp.arange(steps_new)[:, None])[None, None, None]
    old_scores = jnp.where(old_mask, old_scores, neg_fill)
    new_scores = jnp.where(new_mask, new_scores, neg_fill)
    row_max = jnp.maximum(
        jnp.max(old_scores, axis=-1, keepdims=True), jnp.max(new_scores, axis=-1, keepdims=True)
    )
    old_probs = jnp.where(old_mask, jnp.exp(old_scores - row_max), 0.0)
    new_probs = jnp.where(new_mask, jnp.exp(new_scores - row_max), 0.0)
    denom_sum = jnp.sum(old_probs, axis=-1, keepdims=True) + jnp.sum(
        new_probs, axis=-1, keepdims=True
    )
    old_weights = (old_probs / denom_sum).astype(jnp.bfloat16)
    new_weights = (new_probs / denom_sum).astype(jnp.bfloat16)
    attended = jnp.einsum(
        "bkgcs,bskd->bckgd", old_weights, cache_values, preferred_element_type=jnp.float32
    )
    attended = attended + jnp.einsum(
        "bkgct,btkd->bckgd", new_weights, new_kv[:, 1], preferred_element_type=jnp.float32
    )
    return attended.astype(jnp.bfloat16).reshape(branch * steps_new, qheads * head_width)


def parent_listing(fork_parent):
    groups = lax.axis_size("dp")
    slots = fork_parent.shape[0]
    row = jnp.pad(fork_parent, (0, LANES - slots), constant_values=-1)
    copies = jnp.broadcast_to(row[None, None, :], (groups, 1, LANES))
    return lax.all_to_all(copies, "dp", split_axis=0, concat_axis=0, tiled=True)[:, 0]


def shift_z(step):
    return [(z * NY + y, (z + step) % NZ * NY + y) for z in range(NZ) for y in range(NY)]


def groups_far():
    return [[(near + NEAR * far) * NY + y for far in range(NZ // NEAR)] for near in range(NEAR) for y in range(NY)]


def groups_y():
    return [[z * NY + y for y in range(NY)] for z in range(NZ)]


def share(block, groups):
    return exchange(jnp.broadcast_to(block[None], (len(groups[0]),) + block.shape), groups)


def exchange(copies, groups):
    return lax.all_to_all(
        copies, "dp", split_axis=0, concat_axis=0, tiled=True, axis_index_groups=groups
    )


def pick_kernel(me_ref, listing_ref, table_ref, cache_ref, out_ref, sems):
    asked = listing_ref[...]
    mine = (asked >> 4) == me_ref[0]
    rows = asked & (BR_DEV - 1)
    lowest = jnp.min(jnp.where(mine, rows, BR_DEV - 1))
    highest = jnp.max(jnp.where(mine, rows, 0))
    copies = []
    for which, row in enumerate((lowest, highest)):
        for page in range(PAGES):
            copies.append(
                pltpu.make_async_copy(
                    cache_ref.at[table_ref[row, page]], out_ref.at[which, page], sems.at[which, page]
                )
            )
    for copy in copies:
        copy.start()
    for copy in copies:
        copy.wait()


def pick_pages(me_index, listing, page_table, cache):
    return pl.pallas_call(
        pick_kernel,
        out_shape=jax.ShapeDtypeStruct((2, PAGES) + cache.shape[1:], cache.dtype),
        in_specs=[
            pl.BlockSpec(memory_space=pltpu.SMEM),
            pl.BlockSpec(memory_space=pltpu.VMEM),
            pl.BlockSpec(memory_space=pltpu.SMEM),
            pl.BlockSpec(memory_space=pl.ANY),
        ],
        out_specs=pl.BlockSpec(memory_space=pltpu.VMEM),
        scratch_shapes=[pltpu.SemaphoreType.DMA((2, PAGES))],
    )(me_index.reshape(1), listing, page_table, cache)


def place_kernel(count, aliased, where_ref, *refs):
    sources = refs[:count]
    out_ref, held, load_sems, sems = refs[count + aliased :]
    slots = out_ref.shape[0]
    loads, base = [], 0
    for number, source in enumerate(sources):
        size = source.shape[0]
        loads.append(
            pltpu.make_async_copy(source, held.at[pl.ds(base, size)], load_sems.at[number])
        )
        base += size
    for load in loads:
        load.start()
    for load in loads:
        load.wait()

    @pl.loop(0, slots)
    def _(slot):
        where = where_ref[slot]

        @pl.when(where >= 0)
        def _():
            pltpu.make_async_copy(held.at[where], out_ref.at[slot], sems.at[slot]).start()

    @pl.loop(0, slots)
    def _(slot):
        @pl.when(where_ref[slot] >= 0)
        def _():
            pltpu.make_async_copy(held.at[0], out_ref.at[slot], sems.at[slot]).wait()


def place_children(where, sources, earlier=None):
    slots = where.shape[0]
    count = len(sources)
    blocks = sum(source.shape[0] for source in sources)
    tile = sources[0].shape[1:]
    given = [where] + list(sources) + ([] if earlier is None else [earlier])
    return pl.pallas_call(
        functools.partial(place_kernel, count, len(given) - 1 - count),
        out_shape=jax.ShapeDtypeStruct((slots,) + tile, sources[0].dtype),
        in_specs=[pl.BlockSpec(memory_space=pltpu.SMEM)]
        + [pl.BlockSpec(memory_space=pl.ANY)] * (len(given) - 1),
        out_specs=pl.BlockSpec(memory_space=pl.ANY),
        scratch_shapes=[
            pltpu.VMEM((blocks,) + tile, sources[0].dtype),
            pltpu.SemaphoreType.DMA((count,)),
            pltpu.SemaphoreType.DMA((slots,)),
        ],
        input_output_aliases={} if earlier is None else {len(given) - 1: 0},
        compiler_params=pltpu.CompilerParams(vmem_limit_bytes=24 * 2**20),
    )(*given)


def child_places(listing, fork_parent, me_index):
    owner = fork_parent // BR_DEV
    asked = listing.reshape(1, -1)
    same = (asked // BR_DEV) == owner[:, None]
    first = jnp.min(jnp.where(same, asked % BR_DEV, BR_DEV - 1), axis=1)
    is_low = fork_parent % BR_DEV == first
    owner_z, owner_y = owner // NY, owner % NY
    far = owner_z // NEAR
    near = (me_index // NY - owner_z) % NEAR
    in_plane = owner_y * (NZ // NEAR) + far
    step = jnp.where(near == 0, 0, jnp.where(near == 1, NZ, 2 * NZ))
    early = jnp.where(is_low | (near == 2), -1, step + in_plane)
    in_all = (owner_y * NEAR + near) * (NZ // NEAR) + far
    late = jnp.where(is_low, NZ + in_all, jnp.where(near == 2, in_plane, -1))
    return early.astype(jnp.int32), late.astype(jnp.int32)


def gather_far(listing, kv_cache, page_table):
    cache = kv_cache[:, :, :, 0]
    width = cache.shape[-1]
    picked = pick_pages(lax.axis_index("dp"), listing, page_table, cache)
    rows = picked[0].size // width
    return share(picked.reshape(2 * rows, width), groups_far()), picked.shape[1:]


def gather_near(far):
    rows, width = far.shape[1] // 2, far.shape[2]
    low_far = far[:, :rows].reshape(-1, width)
    high_far = far[:, rows:].reshape(-1, width)
    copies = jnp.broadcast_to(high_far[None], (NY,) + high_far.shape)
    low_far, copies = lax.optimization_barrier((low_far, copies))
    high_plane = exchange(copies, groups_y()).reshape(-1, width)
    low_column = jnp.concatenate(
        [low_far] + [lax.ppermute(low_far, "dp", shift_z(step)) for step in (1, 2, -1)]
    )
    return low_column, high_plane


def gather_rest(low_column, high_plane):
    half = high_plane.shape[0] // 2
    low_all = share(low_column, groups_y())
    up = lax.ppermute(high_plane, "dp", shift_z(1))
    down = lax.ppermute(high_plane, "dp", shift_z(-1))
    up_two = lax.ppermute(high_plane[:half], "dp", shift_z(2))
    down_two = lax.ppermute(high_plane[half:], "dp", shift_z(-2))
    return (high_plane, up, down), (up_two, down_two, low_all)


def halve(held, apart):
    shards = lax.axis_size("tensor")
    mine = (lax.axis_index("tensor") // apart) % 2
    pairs = held.reshape((-1, 2) + held.shape[1:])
    keep = lax.dynamic_index_in_dim(pairs, mine, 1, keepdims=False)
    send = lax.dynamic_index_in_dim(pairs, 1 - mine, 1, keepdims=False)
    came = lax.ppermute(send, "tensor", [(i, i ^ apart) for i in range(shards)])
    return keep.astype(jnp.float32) + came.astype(jnp.float32)


def local(
    queries,
    new_kv,
    kv_cache,
    page_table,
    lengths,
    out_proj,
    residual,
    norm_gain,
    score_weight,
    fork_parent,
):
    listing, queries = lax.optimization_barrier((parent_listing(fork_parent), queries))
    attended = attend(queries, new_kv, kv_cache, page_table, lengths)
    rows_here = residual.shape[0]
    partial = jnp.dot(attended, out_proj, preferred_element_type=jnp.float32).astype(jnp.bfloat16)
    far, tile = gather_far(listing, kv_cache, page_table)
    held = halve(partial.reshape(lax.axis_size("tensor"), rows_here, -1), 1).astype(jnp.bfloat16)
    far, held = lax.optimization_barrier((far, held))
    low_column, high_plane = gather_near(far)
    held = halve(held, 2).astype(jnp.bfloat16)
    low_column, high_plane, held = lax.optimization_barrier((low_column, high_plane, held))
    first, last = gather_rest(low_column, high_plane)
    early, late = child_places(listing, fork_parent, lax.axis_index("dp"))
    placed = place_children(early, [part.reshape((-1,) + tile) for part in first])
    placed = place_children(late, [part.reshape((-1,) + tile) for part in last], placed)
    child_pages = placed[:, :, :, :, None]
    updated = halve(held, 4)[0] + residual.astype(jnp.float32)
    hidden_out = updated.astype(jnp.bfloat16)
    block_ends = updated.reshape(rows_here // CH, CH, updated.shape[1])[:, CH - 1]
    normed = (
        block_ends
        * lax.rsqrt(jnp.mean(block_ends * block_ends, axis=-1, keepdims=True) + 1e-06)
        * norm_gain.astype(jnp.float32)
    )
    scores = jax.nn.sigmoid(jnp.sum(normed * score_weight.astype(jnp.float32), axis=-1))
    return (hidden_out, scores, child_pages)


def solution(mesh):
    in_specs = (
        P("dp", None, "tensor", None),
        P("dp", None, None, "tensor", None),
        P("dp", None, None, "tensor", None),
        P("dp", None),
        P("dp"),
        P("tensor", None),
        P(("dp", "tensor"), None),
        P(),
        P(),
        P("dp"),
    )
    out_specs = (
        P(("dp", "tensor"), None),
        P(("dp", "tensor")),
        P("dp", None, None, None, "tensor", None),
    )
    return jax.shard_map(local, mesh=mesh, in_specs=in_specs, out_specs=out_specs, check_vma=False)
```

```python
import functools

import jax
import jax.numpy as jnp
from jax import lax
from jax.experimental import pallas as pl
from jax.experimental.pallas import tpu as pltpu
from jax.sharding import PartitionSpec as P

BR_DEV = 16
CH = 16
PAGE = 16
PREFIX = 128
PAGES = PREFIX // PAGE
NZ, NY = 16, 4
NEAR = 4
FRONT = 6
LANES = 128


neg_fill = -1e30

def attend(queries, new_kv, kv_cache, page_table, lengths):
    branch, steps_new, qheads, head_width = queries.shape
    kvheads = new_kv.shape[3]
    per_group = qheads // kvheads
    cache_pages = kv_cache[page_table]
    key_span = cache_pages.shape[1] * cache_pages.shape[3]
    cache_keys = cache_pages[:, :, 0].reshape(branch, key_span, kvheads, head_width)
    cache_values = cache_pages[:, :, 1].reshape(branch, key_span, kvheads, head_width)
    grouped = queries.reshape(branch, steps_new, kvheads, per_group, head_width)
    score_scale = head_width ** (-0.5)
    old_scores = (
        jnp.einsum("bckgd,bskd->bkgcs", grouped, cache_keys, preferred_element_type=jnp.float32)
        * score_scale
    )
    new_scores = (
        jnp.einsum("bckgd,btkd->bkgct", grouped, new_kv[:, 0], preferred_element_type=jnp.float32)
        * score_scale
    )
    old_mask = (jnp.arange(key_span)[None, :] < lengths[:, None])[:, None, None, None, :]
    new_mask = (jnp.arange(steps_new)[None, :] <= jnp.arange(steps_new)[:, None])[None, None, None]
    old_scores = jnp.where(old_mask, old_scores, neg_fill)
    new_scores = jnp.where(new_mask, new_scores, neg_fill)
    row_max = jnp.maximum(
        jnp.max(old_scores, axis=-1, keepdims=True), jnp.max(new_scores, axis=-1, keepdims=True)
    )
    old_probs = jnp.where(old_mask, jnp.exp(old_scores - row_max), 0.0)
    new_probs = jnp.where(new_mask, jnp.exp(new_scores - row_max), 0.0)
    denom_sum = jnp.sum(old_probs, axis=-1, keepdims=True) + jnp.sum(
        new_probs, axis=-1, keepdims=True
    )
    old_weights = (old_probs / denom_sum).astype(jnp.bfloat16)
    new_weights = (new_probs / denom_sum).astype(jnp.bfloat16)
    attended = jnp.einsum(
        "bkgcs,bskd->bckgd", old_weights, cache_values, preferred_element_type=jnp.float32
    )
    attended = attended + jnp.einsum(
        "bkgct,btkd->bckgd", new_weights, new_kv[:, 1], preferred_element_type=jnp.float32
    )
    return attended.astype(jnp.bfloat16).reshape(branch * steps_new, qheads * head_width)


def parent_listing(fork_parent):
    groups = lax.axis_size("dp")
    slots = fork_parent.shape[0]
    row = jnp.pad(fork_parent, (0, LANES - slots), constant_values=-1)
    copies = jnp.broadcast_to(row[None, None, :], (groups, 1, LANES))
    return lax.all_to_all(copies, "dp", split_axis=0, concat_axis=0, tiled=True)[:, 0]


def shift_z(step):
    return [(z * NY + y, (z + step) % NZ * NY + y) for z in range(NZ) for y in range(NY)]


def groups_far():
    return [[(near + NEAR * far) * NY + y for far in range(NZ // NEAR)] for near in range(NEAR) for y in range(NY)]


def groups_z():
    return [[z * NY + y for z in range(NZ)] for y in range(NY)]


def groups_y():
    return [[z * NY + y for y in range(NY)] for z in range(NZ)]


def share(block, groups):
    copies = jnp.broadcast_to(block[None], (len(groups[0]),) + block.shape)
    return lax.all_to_all(
        copies, "dp", split_axis=0, concat_axis=0, tiled=True, axis_index_groups=groups
    )


def pick_kernel(me_ref, listing_ref, table_ref, cache_ref, front_ref, back_ref, sems):
    asked = listing_ref[...]
    mine = (asked >> 4) == me_ref[0]
    rows = asked & (BR_DEV - 1)
    lowest = jnp.min(jnp.where(mine, rows, BR_DEV - 1))
    highest = jnp.max(jnp.where(mine, rows, 0))
    copies = []
    for which, row in enumerate((lowest, highest)):
        for page in range(PAGES):
            target = front_ref.at[which, page] if page < FRONT else back_ref.at[which, page - FRONT]
            copies.append(
                pltpu.make_async_copy(
                    cache_ref.at[table_ref[row, page]], target, sems.at[which, page]
                )
            )
    for copy in copies:
        copy.start()
    for copy in copies:
        copy.wait()


def pick_pages(me_index, listing, page_table, cache):
    return pl.pallas_call(
        pick_kernel,
        out_shape=tuple(
            jax.ShapeDtypeStruct((2, pages) + cache.shape[1:], cache.dtype)
            for pages in (FRONT, PAGES - FRONT)
        ),
        in_specs=[
            pl.BlockSpec(memory_space=pltpu.SMEM),
            pl.BlockSpec(memory_space=pltpu.VMEM),
            pl.BlockSpec(memory_space=pltpu.SMEM),
            pl.BlockSpec(memory_space=pl.ANY),
        ],
        out_specs=(pl.BlockSpec(memory_space=pltpu.VMEM),) * 2,
        scratch_shapes=[pltpu.SemaphoreType.DMA((2, PAGES))],
    )(me_index.reshape(1), listing, page_table, cache)


def place_kernel(first_page, aliased, where_ref, source_ref, *refs):
    out_ref, sems = refs[aliased:]
    slots = out_ref.shape[0]
    pages = source_ref.shape[1]

    def store(slot):
        return pltpu.make_async_copy(
            source_ref.at[where_ref[slot]], out_ref.at[slot, pl.ds(first_page, pages)], sems.at[slot]
        )

    @pl.loop(0, slots)
    def _(slot):
        store(slot).start()

    @pl.loop(0, slots)
    def _(slot):
        store(slot).wait()


def place_children(where, source, first_page, earlier=None):
    slots = where.shape[0]
    given = [where, source] + ([] if earlier is None else [earlier])
    return pl.pallas_call(
        functools.partial(place_kernel, first_page, len(given) - 2),
        out_shape=jax.ShapeDtypeStruct((slots, PAGES) + source.shape[2:], source.dtype),
        in_specs=[
            pl.BlockSpec(memory_space=pltpu.SMEM),
            pl.BlockSpec(memory_space=pltpu.VMEM),
        ]
        + [pl.BlockSpec(memory_space=pl.ANY)] * (len(given) - 2),
        out_specs=pl.BlockSpec(memory_space=pl.ANY),
        scratch_shapes=[pltpu.SemaphoreType.DMA((slots,))],
        input_output_aliases={} if earlier is None else {2: 0},
        compiler_params=pltpu.CompilerParams(vmem_limit_bytes=24 * 2**20),
    )(*given)


def child_places(listing, fork_parent, me_index):
    owner = fork_parent // BR_DEV
    asked = listing.reshape(1, -1)
    same = (asked // BR_DEV) == owner[:, None]
    first = jnp.min(jnp.where(same, asked % BR_DEV, BR_DEV - 1), axis=1)
    which = (fork_parent % BR_DEV != first).astype(jnp.int32)
    owner_z, owner_y = owner // NY, owner % NY
    near = (me_index // NY - owner_z) % NEAR
    front = owner * 2 + which
    back = ((owner_y * NEAR + near) * (NZ // NEAR) + owner_z // NEAR) * 2 + which
    return front, back


def gather_fronts(front):
    width = front.shape[-1]
    plane = share(front.reshape(-1, width), groups_y()).reshape(-1, width)
    fronts = lax.all_gather(plane, "dp", axis=0, tiled=True, axis_index_groups=groups_z())
    return fronts.reshape((-1,) + front.shape[1:])


def gather_backs_far(back):
    width = back.shape[-1]
    return share(back.reshape(-1, width), groups_far()).reshape(-1, width)


def gather_backs_near(far):
    return jnp.concatenate(
        [far] + [lax.ppermute(far, "dp", shift_z(step)) for step in (1, 2, -1)]
    )


def halve(held, apart):
    shards = lax.axis_size("tensor")
    mine = (lax.axis_index("tensor") // apart) % 2
    pairs = held.reshape((-1, 2) + held.shape[1:])
    keep = lax.dynamic_index_in_dim(pairs, mine, 1, keepdims=False)
    send = lax.dynamic_index_in_dim(pairs, 1 - mine, 1, keepdims=False)
    came = lax.ppermute(send, "tensor", [(i, i ^ apart) for i in range(shards)])
    return keep.astype(jnp.float32) + came.astype(jnp.float32)


def local(
    queries,
    new_kv,
    kv_cache,
    page_table,
    lengths,
    out_proj,
    residual,
    norm_gain,
    score_weight,
    fork_parent,
):
    listing, queries = lax.optimization_barrier((parent_listing(fork_parent), queries))
    cache = kv_cache[:, :, :, 0]
    front, back = pick_pages(lax.axis_index("dp"), listing, page_table, cache)
    fronts = gather_fronts(front)
    attended = attend(queries, new_kv, kv_cache, page_table, lengths)
    rows_here = residual.shape[0]
    partial = jnp.dot(attended, out_proj, preferred_element_type=jnp.float32).astype(jnp.bfloat16)
    far, partial = lax.optimization_barrier((gather_backs_far(back), partial))
    held = halve(partial.reshape(lax.axis_size("tensor"), rows_here, -1), 1).astype(jnp.bfloat16)
    column, held = lax.optimization_barrier((gather_backs_near(far), held))
    backs = share(column, groups_y()).reshape((-1,) + back.shape[1:])
    held = halve(held, 2).astype(jnp.bfloat16)
    updated = halve(held, 4)[0] + residual.astype(jnp.float32)
    hidden_out = updated.astype(jnp.bfloat16)
    block_ends = updated.reshape(rows_here // CH, CH, updated.shape[1])[:, CH - 1]
    normed = (
        block_ends
        * lax.rsqrt(jnp.mean(block_ends * block_ends, axis=-1, keepdims=True) + 1e-06)
        * norm_gain.astype(jnp.float32)
    )
    scores = jax.nn.sigmoid(jnp.sum(normed * score_weight.astype(jnp.float32), axis=-1))
    front_at, back_at = child_places(listing, fork_parent, lax.axis_index("dp"))
    child_pages = place_children(back_at, backs, FRONT)
    child_pages = place_children(front_at, fronts, 0, child_pages)[:, :, :, :, None]
    return (hidden_out, scores, child_pages)


def solution(mesh):
    in_specs = (
        P("dp", None, "tensor", None),
        P("dp", None, None, "tensor", None),
        P("dp", None, None, "tensor", None),
        P("dp", None),
        P("dp"),
        P("tensor", None),
        P(("dp", "tensor"), None),
        P(),
        P(),
        P("dp"),
    )
    out_specs = (
        P(("dp", "tensor"), None),
        P(("dp", "tensor")),
        P("dp", None, None, None, "tensor", None),
    )
    return jax.shard_map(local, mesh=mesh, in_specs=in_specs, out_specs=out_specs, check_vma=False)
```

```python
import functools

import jax
import jax.numpy as jnp
from jax import lax
from jax.experimental import pallas as pl
from jax.experimental.pallas import tpu as pltpu
from jax.sharding import PartitionSpec as P

BR_DEV = 16
CH = 16
PAGE = 16
PREFIX = 128
PAGES = PREFIX // PAGE
NZ, NY = 16, 4
NEAR = 4
FRONT = 5
LANES = 128


neg_fill = -1e30

def cached(kv_cache, page_table):
    pages = kv_cache[page_table]
    branch, count, _, page, kvheads, head_width = pages.shape
    flat = (branch, count * page, kvheads, head_width)
    return pages[:, :, 0].reshape(flat), pages[:, :, 1].reshape(flat)


def attend(queries, new_kv, cache_keys, cache_values, lengths):
    branch, steps_new, qheads, head_width = queries.shape
    kvheads = new_kv.shape[3]
    per_group = qheads // kvheads
    key_span = cache_keys.shape[1]
    grouped = queries.reshape(branch, steps_new, kvheads, per_group, head_width)
    score_scale = head_width ** (-0.5)
    old_scores = (
        jnp.einsum("bckgd,bskd->bkgcs", grouped, cache_keys, preferred_element_type=jnp.float32)
        * score_scale
    )
    new_scores = (
        jnp.einsum("bckgd,btkd->bkgct", grouped, new_kv[:, 0], preferred_element_type=jnp.float32)
        * score_scale
    )
    old_mask = (jnp.arange(key_span)[None, :] < lengths[:, None])[:, None, None, None, :]
    new_mask = (jnp.arange(steps_new)[None, :] <= jnp.arange(steps_new)[:, None])[None, None, None]
    old_scores = jnp.where(old_mask, old_scores, neg_fill)
    new_scores = jnp.where(new_mask, new_scores, neg_fill)
    row_max = jnp.maximum(
        jnp.max(old_scores, axis=-1, keepdims=True), jnp.max(new_scores, axis=-1, keepdims=True)
    )
    old_probs = jnp.where(old_mask, jnp.exp(old_scores - row_max), 0.0)
    new_probs = jnp.where(new_mask, jnp.exp(new_scores - row_max), 0.0)
    denom_sum = jnp.sum(old_probs, axis=-1, keepdims=True) + jnp.sum(
        new_probs, axis=-1, keepdims=True
    )
    old_weights = (old_probs / denom_sum).astype(jnp.bfloat16)
    new_weights = (new_probs / denom_sum).astype(jnp.bfloat16)
    attended = jnp.einsum(
        "bkgcs,bskd->bckgd", old_weights, cache_values, preferred_element_type=jnp.float32
    )
    attended = attended + jnp.einsum(
        "bkgct,btkd->bckgd", new_weights, new_kv[:, 1], preferred_element_type=jnp.float32
    )
    return attended.astype(jnp.bfloat16).reshape(branch * steps_new, qheads * head_width)


def parent_listing(fork_parent):
    groups = lax.axis_size("dp")
    slots = fork_parent.shape[0]
    row = jnp.pad(fork_parent, (0, LANES - slots), constant_values=-1)
    copies = jnp.broadcast_to(row[None, None, :], (groups, 1, LANES))
    return lax.all_to_all(copies, "dp", split_axis=0, concat_axis=0, tiled=True)[:, 0]


def shift_z(step):
    return [(z * NY + y, (z + step) % NZ * NY + y) for z in range(NZ) for y in range(NY)]


def groups_far():
    return [[(near + NEAR * far) * NY + y for far in range(NZ // NEAR)] for near in range(NEAR) for y in range(NY)]


def groups_z():
    return [[z * NY + y for z in range(NZ)] for y in range(NY)]


def groups_y():
    return [[z * NY + y for y in range(NY)] for z in range(NZ)]


def share(block, groups):
    copies = jnp.broadcast_to(block[None], (len(groups[0]),) + block.shape)
    return lax.all_to_all(
        copies, "dp", split_axis=0, concat_axis=0, tiled=True, axis_index_groups=groups
    )


def pick_kernel(me_ref, listing_ref, table_ref, cache_ref, front_ref, back_ref, sems):
    asked = listing_ref[...]
    mine = (asked >> 4) == me_ref[0]
    rows = asked & (BR_DEV - 1)
    lowest = jnp.min(jnp.where(mine, rows, BR_DEV - 1))
    highest = jnp.max(jnp.where(mine, rows, 0))
    copies = []
    for which, row in enumerate((lowest, highest)):
        for page in range(PAGES):
            target = front_ref.at[which, page] if page < FRONT else back_ref.at[which, page - FRONT]
            copies.append(
                pltpu.make_async_copy(
                    cache_ref.at[table_ref[row, page]], target, sems.at[which, page]
                )
            )
    for copy in copies:
        copy.start()
    for copy in copies:
        copy.wait()


def pick_pages(me_index, listing, page_table, cache):
    return pl.pallas_call(
        pick_kernel,
        out_shape=tuple(
            jax.ShapeDtypeStruct((2, pages) + cache.shape[1:], cache.dtype)
            for pages in (FRONT, PAGES - FRONT)
        ),
        in_specs=[
            pl.BlockSpec(memory_space=pltpu.SMEM),
            pl.BlockSpec(memory_space=pltpu.VMEM),
            pl.BlockSpec(memory_space=pltpu.SMEM),
            pl.BlockSpec(memory_space=pl.ANY),
        ],
        out_specs=(pl.BlockSpec(memory_space=pltpu.VMEM),) * 2,
        scratch_shapes=[pltpu.SemaphoreType.DMA((2, PAGES))],
    )(me_index.reshape(1), listing, page_table, cache)


def place_kernel(first_page, aliased, where_ref, source_ref, *refs):
    out_ref, sems = refs[aliased:]
    slots = out_ref.shape[0]
    pages = source_ref.shape[1]

    def store(slot):
        return pltpu.make_async_copy(
            source_ref.at[where_ref[slot]], out_ref.at[slot, pl.ds(first_page, pages)], sems.at[slot]
        )

    @pl.loop(0, slots)
    def _(slot):
        store(slot).start()

    @pl.loop(0, slots)
    def _(slot):
        store(slot).wait()


def place_children(where, source, first_page, earlier=None):
    slots = where.shape[0]
    given = [where, source] + ([] if earlier is None else [earlier])
    return pl.pallas_call(
        functools.partial(place_kernel, first_page, len(given) - 2),
        out_shape=jax.ShapeDtypeStruct((slots, PAGES) + source.shape[2:], source.dtype),
        in_specs=[
            pl.BlockSpec(memory_space=pltpu.SMEM),
            pl.BlockSpec(memory_space=pltpu.VMEM),
        ]
        + [pl.BlockSpec(memory_space=pl.ANY)] * (len(given) - 2),
        out_specs=pl.BlockSpec(memory_space=pl.ANY),
        scratch_shapes=[pltpu.SemaphoreType.DMA((slots,))],
        input_output_aliases={} if earlier is None else {2: 0},
        compiler_params=pltpu.CompilerParams(vmem_limit_bytes=24 * 2**20),
    )(*given)


def child_places(listing, fork_parent, me_index):
    owner = fork_parent // BR_DEV
    asked = listing.reshape(1, -1)
    same = (asked // BR_DEV) == owner[:, None]
    first = jnp.min(jnp.where(same, asked % BR_DEV, BR_DEV - 1), axis=1)
    which = (fork_parent % BR_DEV != first).astype(jnp.int32)
    owner_z, owner_y = owner // NY, owner % NY
    near = (me_index // NY - owner_z) % NEAR
    front = owner * 2 + which
    back = ((owner_y * NEAR + near) * (NZ // NEAR) + owner_z // NEAR) * 2 + which
    return front, back


def gather_fronts(front):
    width = front.shape[-1]
    plane = share(front.reshape(-1, width), groups_y()).reshape(-1, width)
    fronts = lax.all_gather(plane, "dp", axis=0, tiled=True, axis_index_groups=groups_z())
    return fronts.reshape((-1,) + front.shape[1:])


def gather_backs_far(back):
    width = back.shape[-1]
    return share(back.reshape(-1, width), groups_far()).reshape(-1, width)


def gather_backs_near(far):
    return jnp.concatenate(
        [far] + [lax.ppermute(far, "dp", shift_z(step)) for step in (1, 2, -1)]
    )


def halve(held, apart):
    shards = lax.axis_size("tensor")
    mine = (lax.axis_index("tensor") // apart) % 2
    pairs = held.reshape((-1, 2) + held.shape[1:])
    keep = lax.dynamic_index_in_dim(pairs, mine, 1, keepdims=False)
    send = lax.dynamic_index_in_dim(pairs, 1 - mine, 1, keepdims=False)
    came = lax.ppermute(send, "tensor", [(i, i ^ apart) for i in range(shards)])
    return keep.astype(jnp.float32) + came.astype(jnp.float32)


def local(
    queries,
    new_kv,
    kv_cache,
    page_table,
    lengths,
    out_proj,
    residual,
    norm_gain,
    score_weight,
    fork_parent,
):
    keys, values = cached(kv_cache, page_table)
    listing, queries, keys, values = lax.optimization_barrier(
        (parent_listing(fork_parent), queries, keys, values)
    )
    cache = kv_cache[:, :, :, 0]
    front, back = pick_pages(lax.axis_index("dp"), listing, page_table, cache)
    fronts = gather_fronts(front)
    attended = attend(queries, new_kv, keys, values, lengths)
    rows_here = residual.shape[0]
    partial = jnp.dot(attended, out_proj, preferred_element_type=jnp.float32).astype(jnp.bfloat16)
    far, partial = lax.optimization_barrier((gather_backs_far(back), partial))
    held = halve(partial.reshape(lax.axis_size("tensor"), rows_here, -1), 1).astype(jnp.bfloat16)
    column, held = lax.optimization_barrier((gather_backs_near(far), held))
    backs = share(column, groups_y()).reshape((-1,) + back.shape[1:])
    held = halve(held, 2).astype(jnp.bfloat16)
    updated = halve(held, 4)[0] + residual.astype(jnp.float32)
    hidden_out = updated.astype(jnp.bfloat16)
    block_ends = updated.reshape(rows_here // CH, CH, updated.shape[1])[:, CH - 1]
    normed = (
        block_ends
        * lax.rsqrt(jnp.mean(block_ends * block_ends, axis=-1, keepdims=True) + 1e-06)
        * norm_gain.astype(jnp.float32)
    )
    scores = jax.nn.sigmoid(jnp.sum(normed * score_weight.astype(jnp.float32), axis=-1))
    front_at, back_at = child_places(listing, fork_parent, lax.axis_index("dp"))
    child_pages = place_children(back_at, backs, FRONT)
    child_pages = place_children(front_at, fronts, 0, child_pages)[:, :, :, :, None]
    return (hidden_out, scores, child_pages)


def solution(mesh):
    in_specs = (
        P("dp", None, "tensor", None),
        P("dp", None, None, "tensor", None),
        P("dp", None, None, "tensor", None),
        P("dp", None),
        P("dp"),
        P("tensor", None),
        P(("dp", "tensor"), None),
        P(),
        P(),
        P("dp"),
    )
    out_specs = (
        P(("dp", "tensor"), None),
        P(("dp", "tensor")),
        P("dp", None, None, None, "tensor", None),
    )
    return jax.shard_map(local, mesh=mesh, in_specs=in_specs, out_specs=out_specs, check_vma=False)
```

```python
import functools

import jax
import jax.numpy as jnp
from jax import lax
from jax.experimental import pallas as pl
from jax.experimental.pallas import tpu as pltpu
from jax.sharding import PartitionSpec as P

BR_DEV = 16
CH = 16
PAGE = 16
PREFIX = 128
PAGES = PREFIX // PAGE
NZ, NY = 16, 4
NEAR = 4
LANES = 128


neg_fill = -1e30

def cached(kv_cache, page_table):
    pages = kv_cache[page_table]
    branch, count, _, page, kvheads, head_width = pages.shape
    flat = (branch, count * page, kvheads, head_width)
    return pages[:, :, 0].reshape(flat), pages[:, :, 1].reshape(flat)


def attend(queries, new_kv, cache_keys, cache_values, lengths):
    branch, steps_new, qheads, head_width = queries.shape
    kvheads = new_kv.shape[3]
    per_group = qheads // kvheads
    key_span = cache_keys.shape[1]
    grouped = queries.reshape(branch, steps_new, kvheads, per_group, head_width)
    score_scale = head_width ** (-0.5)
    old_scores = (
        jnp.einsum("bckgd,bskd->bkgcs", grouped, cache_keys, preferred_element_type=jnp.float32)
        * score_scale
    )
    new_scores = (
        jnp.einsum("bckgd,btkd->bkgct", grouped, new_kv[:, 0], preferred_element_type=jnp.float32)
        * score_scale
    )
    old_mask = (jnp.arange(key_span)[None, :] < lengths[:, None])[:, None, None, None, :]
    new_mask = (jnp.arange(steps_new)[None, :] <= jnp.arange(steps_new)[:, None])[None, None, None]
    old_scores = jnp.where(old_mask, old_scores, neg_fill)
    new_scores = jnp.where(new_mask, new_scores, neg_fill)
    row_max = jnp.maximum(
        jnp.max(old_scores, axis=-1, keepdims=True), jnp.max(new_scores, axis=-1, keepdims=True)
    )
    old_probs = jnp.where(old_mask, jnp.exp(old_scores - row_max), 0.0)
    new_probs = jnp.where(new_mask, jnp.exp(new_scores - row_max), 0.0)
    denom_sum = jnp.sum(old_probs, axis=-1, keepdims=True) + jnp.sum(
        new_probs, axis=-1, keepdims=True
    )
    old_weights = (old_probs / denom_sum).astype(jnp.bfloat16)
    new_weights = (new_probs / denom_sum).astype(jnp.bfloat16)
    attended = jnp.einsum(
        "bkgcs,bskd->bckgd", old_weights, cache_values, preferred_element_type=jnp.float32
    )
    attended = attended + jnp.einsum(
        "bkgct,btkd->bckgd", new_weights, new_kv[:, 1], preferred_element_type=jnp.float32
    )
    return attended.astype(jnp.bfloat16).reshape(branch * steps_new, qheads * head_width)


def parent_listing(fork_parent):
    groups = lax.axis_size("dp")
    slots = fork_parent.shape[0]
    row = jnp.pad(fork_parent, (0, LANES - slots), constant_values=-1)
    copies = jnp.broadcast_to(row[None, None, :], (groups, 1, LANES))
    return lax.all_to_all(copies, "dp", split_axis=0, concat_axis=0, tiled=True)[:, 0]


def shift_z(step):
    return [(z * NY + y, (z + step) % NZ * NY + y) for z in range(NZ) for y in range(NY)]


def groups_far():
    return [[(near + NEAR * far) * NY + y for far in range(NZ // NEAR)] for near in range(NEAR) for y in range(NY)]


def groups_y():
    return [[z * NY + y for y in range(NY)] for z in range(NZ)]


def share(block, groups):
    return exchange(jnp.broadcast_to(block[None], (len(groups[0]),) + block.shape), groups)


def exchange(copies, groups):
    return lax.all_to_all(
        copies, "dp", split_axis=0, concat_axis=0, tiled=True, axis_index_groups=groups
    )


def pick_kernel(me_ref, listing_ref, table_ref, cache_ref, out_ref, sems):
    copies_wanted = out_ref.shape[0]
    asked = listing_ref[...]
    mine = (asked >> 4) == me_ref[0]
    rows = asked & (BR_DEV - 1)
    lowest = jnp.min(jnp.where(mine, rows, BR_DEV - 1))
    highest = jnp.max(jnp.where(mine, rows, 0))
    copies = []
    for which, row in enumerate((lowest, highest)):
        for page in range(PAGES):
            copies.append(
                pltpu.make_async_copy(
                    cache_ref.at[table_ref[row, page]], out_ref.at[0, which, page], sems.at[which, page]
                )
            )
    for copy in copies:
        copy.start()
    for copy in copies:
        copy.wait()
    for number in range(1, copies_wanted):
        out_ref[number] = out_ref[0]


def pick_pages(me_index, listing, page_table, cache, copies):
    return pl.pallas_call(
        pick_kernel,
        out_shape=jax.ShapeDtypeStruct((copies, 2, PAGES) + cache.shape[1:], cache.dtype),
        in_specs=[
            pl.BlockSpec(memory_space=pltpu.SMEM),
            pl.BlockSpec(memory_space=pltpu.VMEM),
            pl.BlockSpec(memory_space=pltpu.SMEM),
            pl.BlockSpec(memory_space=pl.ANY),
        ],
        out_specs=pl.BlockSpec(memory_space=pltpu.VMEM),
        scratch_shapes=[pltpu.SemaphoreType.DMA((2, PAGES))],
    )(me_index.reshape(1), listing, page_table, cache)


def place_kernel(count, aliased, where_ref, *refs):
    sources = refs[:count]
    out_ref, held, load_sems, sems = refs[count + aliased :]
    slots = out_ref.shape[0]
    loads, base = [], 0
    for number, source in enumerate(sources):
        size = source.shape[0]
        loads.append(
            pltpu.make_async_copy(source, held.at[pl.ds(base, size)], load_sems.at[number])
        )
        base += size
    for load in loads:
        load.start()
    for load in loads:
        load.wait()

    @pl.loop(0, slots)
    def _(slot):
        where = where_ref[slot]

        @pl.when(where >= 0)
        def _():
            pltpu.make_async_copy(held.at[where], out_ref.at[slot], sems.at[slot]).start()

    @pl.loop(0, slots)
    def _(slot):
        @pl.when(where_ref[slot] >= 0)
        def _():
            pltpu.make_async_copy(held.at[0], out_ref.at[slot], sems.at[slot]).wait()


def place_children(where, sources, earlier=None):
    slots = where.shape[0]
    count = len(sources)
    blocks = sum(source.shape[0] for source in sources)
    tile = sources[0].shape[1:]
    given = [where] + list(sources) + ([] if earlier is None else [earlier])
    return pl.pallas_call(
        functools.partial(place_kernel, count, len(given) - 1 - count),
        out_shape=jax.ShapeDtypeStruct((slots,) + tile, sources[0].dtype),
        in_specs=[pl.BlockSpec(memory_space=pltpu.SMEM)]
        + [pl.BlockSpec(memory_space=pl.ANY)] * (len(given) - 1),
        out_specs=pl.BlockSpec(memory_space=pl.ANY),
        scratch_shapes=[
            pltpu.VMEM((blocks,) + tile, sources[0].dtype),
            pltpu.SemaphoreType.DMA((count,)),
            pltpu.SemaphoreType.DMA((slots,)),
        ],
        input_output_aliases={} if earlier is None else {len(given) - 1: 0},
        compiler_params=pltpu.CompilerParams(vmem_limit_bytes=24 * 2**20),
    )(*given)


def child_places(listing, fork_parent, me_index):
    owner = fork_parent // BR_DEV
    asked = listing.reshape(1, -1)
    same = (asked // BR_DEV) == owner[:, None]
    first = jnp.min(jnp.where(same, asked % BR_DEV, BR_DEV - 1), axis=1)
    is_low = fork_parent % BR_DEV == first
    owner_z, owner_y = owner // NY, owner % NY
    far = owner_z // NEAR
    near = (me_index // NY - owner_z) % NEAR
    in_plane = owner_y * (NZ // NEAR) + far
    step = jnp.where(near == 0, 0, jnp.where(near == 1, NZ, 2 * NZ))
    early = jnp.where(is_low | (near == 2), -1, step + in_plane)
    in_all = (owner_y * NEAR + near) * (NZ // NEAR) + far
    late = jnp.where(is_low, NZ + in_all, jnp.where(near == 2, in_plane, -1))
    return early.astype(jnp.int32), late.astype(jnp.int32)


def gather_far(picked):
    groups = groups_far()
    return exchange(picked.reshape(len(groups[0]), -1, picked.shape[-1]), groups)


def gather_near(far):
    rows, width = far.shape[1] // 2, far.shape[2]
    low_far = far[:, :rows].reshape(-1, width)
    high_far = far[:, rows:].reshape(-1, width)
    high_plane = share(high_far, groups_y()).reshape(-1, width)
    low_column = jnp.concatenate(
        [low_far] + [lax.ppermute(low_far, "dp", shift_z(step)) for step in (1, 2, -1)]
    )
    return jnp.broadcast_to(low_column[None], (NY,) + low_column.shape), high_plane


def gather_rest(low_copies, high_plane):
    half = high_plane.shape[0] // 2
    low_all = exchange(low_copies, groups_y())
    up = lax.ppermute(high_plane, "dp", shift_z(1))
    down = lax.ppermute(high_plane, "dp", shift_z(-1))
    up_two = lax.ppermute(up[:half], "dp", shift_z(1))
    down_two = lax.ppermute(down[half:], "dp", shift_z(-1))
    return (high_plane, up, down), (up_two, down_two, low_all)


def halve(held, apart):
    shards = lax.axis_size("tensor")
    mine = (lax.axis_index("tensor") // apart) % 2
    pairs = held.reshape((-1, 2) + held.shape[1:])
    keep = lax.dynamic_index_in_dim(pairs, mine, 1, keepdims=False)
    send = lax.dynamic_index_in_dim(pairs, 1 - mine, 1, keepdims=False)
    came = lax.ppermute(send, "tensor", [(i, i ^ apart) for i in range(shards)])
    return keep.astype(jnp.float32) + came.astype(jnp.float32)


def local(
    queries,
    new_kv,
    kv_cache,
    page_table,
    lengths,
    out_proj,
    residual,
    norm_gain,
    score_weight,
    fork_parent,
):
    keys, values = cached(kv_cache, page_table)
    listing, keys, values = lax.optimization_barrier((parent_listing(fork_parent), keys, values))
    cache = kv_cache[:, :, :, 0]
    picked = pick_pages(lax.axis_index("dp"), listing, page_table, cache, NZ // NEAR)
    tile = picked.shape[2:]
    picked, queries = lax.optimization_barrier((picked, queries))
    attended = attend(queries, new_kv, keys, values, lengths)
    rows_here = residual.shape[0]
    partial = jnp.dot(attended, out_proj, preferred_element_type=jnp.float32).astype(jnp.bfloat16)
    held = partial.reshape(lax.axis_size("tensor"), rows_here, -1)
    held = halve(held, 1).astype(jnp.bfloat16)
    far, held = lax.optimization_barrier((gather_far(picked), held))
    held = halve(halve(held, 2).astype(jnp.bfloat16), 4)
    low_copies, high_plane, held = lax.optimization_barrier(gather_near(far) + (held,))
    first, last = gather_rest(low_copies, high_plane)
    early, late = child_places(listing, fork_parent, lax.axis_index("dp"))
    placed = place_children(early, [part.reshape((-1,) + tile) for part in first])
    placed = place_children(late, [part.reshape((-1,) + tile) for part in last], placed)
    child_pages = placed[:, :, :, :, None]
    updated = held[0] + residual.astype(jnp.float32)
    hidden_out = updated.astype(jnp.bfloat16)
    block_ends = updated.reshape(rows_here // CH, CH, updated.shape[1])[:, CH - 1]
    normed = (
        block_ends
        * lax.rsqrt(jnp.mean(block_ends * block_ends, axis=-1, keepdims=True) + 1e-06)
        * norm_gain.astype(jnp.float32)
    )
    scores = jax.nn.sigmoid(jnp.sum(normed * score_weight.astype(jnp.float32), axis=-1))
    return (hidden_out, scores, child_pages)


def solution(mesh):
    in_specs = (
        P("dp", None, "tensor", None),
        P("dp", None, None, "tensor", None),
        P("dp", None, None, "tensor", None),
        P("dp", None),
        P("dp"),
        P("tensor", None),
        P(("dp", "tensor"), None),
        P(),
        P(),
        P("dp"),
    )
    out_specs = (
        P(("dp", "tensor"), None),
        P(("dp", "tensor")),
        P("dp", None, None, None, "tensor", None),
    )
    return jax.shard_map(local, mesh=mesh, in_specs=in_specs, out_specs=out_specs, check_vma=False)
```

```python
import functools

import jax
import jax.numpy as jnp
from jax import lax
from jax.experimental import pallas as pl
from jax.experimental.pallas import tpu as pltpu
from jax.sharding import PartitionSpec as P

BR_DEV = 16
CH = 16
PAGE = 16
PREFIX = 128
PAGES = PREFIX // PAGE
NZ, NY = 16, 4
NEAR = 4
FRONT = 6
LANES = 128


neg_fill = -1e30

def cached(kv_cache, page_table):
    pages = kv_cache[page_table]
    branch, count, _, page, kvheads, head_width = pages.shape
    flat = (branch, count * page, kvheads, head_width)
    return pages[:, :, 0].reshape(flat), pages[:, :, 1].reshape(flat)


def attend(queries, new_kv, cache_keys, cache_values, lengths):
    branch, steps_new, qheads, head_width = queries.shape
    kvheads = new_kv.shape[3]
    per_group = qheads // kvheads
    key_span = cache_keys.shape[1]
    grouped = queries.reshape(branch, steps_new, kvheads, per_group, head_width)
    score_scale = head_width ** (-0.5)
    old_scores = (
        jnp.einsum("bckgd,bskd->bkgcs", grouped, cache_keys, preferred_element_type=jnp.float32)
        * score_scale
    )
    new_scores = (
        jnp.einsum("bckgd,btkd->bkgct", grouped, new_kv[:, 0], preferred_element_type=jnp.float32)
        * score_scale
    )
    old_mask = (jnp.arange(key_span)[None, :] < lengths[:, None])[:, None, None, None, :]
    new_mask = (jnp.arange(steps_new)[None, :] <= jnp.arange(steps_new)[:, None])[None, None, None]
    old_scores = jnp.where(old_mask, old_scores, neg_fill)
    new_scores = jnp.where(new_mask, new_scores, neg_fill)
    row_max = jnp.maximum(
        jnp.max(old_scores, axis=-1, keepdims=True), jnp.max(new_scores, axis=-1, keepdims=True)
    )
    old_probs = jnp.where(old_mask, jnp.exp(old_scores - row_max), 0.0)
    new_probs = jnp.where(new_mask, jnp.exp(new_scores - row_max), 0.0)
    denom_sum = jnp.sum(old_probs, axis=-1, keepdims=True) + jnp.sum(
        new_probs, axis=-1, keepdims=True
    )
    old_weights = (old_probs / denom_sum).astype(jnp.bfloat16)
    new_weights = (new_probs / denom_sum).astype(jnp.bfloat16)
    attended = jnp.einsum(
        "bkgcs,bskd->bckgd", old_weights, cache_values, preferred_element_type=jnp.float32
    )
    attended = attended + jnp.einsum(
        "bkgct,btkd->bckgd", new_weights, new_kv[:, 1], preferred_element_type=jnp.float32
    )
    return attended.astype(jnp.bfloat16).reshape(branch * steps_new, qheads * head_width)


def parent_listing(fork_parent):
    groups = lax.axis_size("dp")
    slots = fork_parent.shape[0]
    row = jnp.pad(fork_parent, (0, LANES - slots), constant_values=-1)
    copies = jnp.broadcast_to(row[None, None, :], (groups, 1, LANES))
    return lax.all_to_all(copies, "dp", split_axis=0, concat_axis=0, tiled=True)[:, 0]


def shift_z(step):
    return [(z * NY + y, (z + step) % NZ * NY + y) for z in range(NZ) for y in range(NY)]


def groups_far():
    return [[(near + NEAR * far) * NY + y for far in range(NZ // NEAR)] for near in range(NEAR) for y in range(NY)]


def groups_z():
    return [[z * NY + y for z in range(NZ)] for y in range(NY)]


def groups_y():
    return [[z * NY + y for y in range(NY)] for z in range(NZ)]


def share(block, groups):
    return exchange(jnp.broadcast_to(block[None], (len(groups[0]),) + block.shape), groups)


def exchange(copies, groups):
    return lax.all_to_all(
        copies, "dp", split_axis=0, concat_axis=0, tiled=True, axis_index_groups=groups
    )


def pick_kernel(me_ref, listing_ref, table_ref, cache_ref, front_ref, back_ref, sems):
    asked = listing_ref[...]
    mine = (asked >> 4) == me_ref[0]
    rows = asked & (BR_DEV - 1)
    lowest = jnp.min(jnp.where(mine, rows, BR_DEV - 1))
    highest = jnp.max(jnp.where(mine, rows, 0))
    copies = []
    for which, row in enumerate((lowest, highest)):
        for page in range(PAGES):
            part, at = (front_ref, page) if page < FRONT else (back_ref, page - FRONT)
            copies.append(
                pltpu.make_async_copy(
                    cache_ref.at[table_ref[row, page]], part.at[0, which, at], sems.at[which, page]
                )
            )
    for copy in copies:
        copy.start()
    for copy in copies:
        copy.wait()
    for part in (front_ref, back_ref):
        for number in range(1, part.shape[0]):
            part[number] = part[0]


def pick_pages(me_index, listing, page_table, cache):
    return pl.pallas_call(
        pick_kernel,
        out_shape=tuple(
            jax.ShapeDtypeStruct((copies, 2, pages) + cache.shape[1:], cache.dtype)
            for copies, pages in ((NY, FRONT), (NZ // NEAR, PAGES - FRONT))
        ),
        in_specs=[
            pl.BlockSpec(memory_space=pltpu.SMEM),
            pl.BlockSpec(memory_space=pltpu.VMEM),
            pl.BlockSpec(memory_space=pltpu.SMEM),
            pl.BlockSpec(memory_space=pl.ANY),
        ],
        out_specs=(pl.BlockSpec(memory_space=pltpu.VMEM),) * 2,
        scratch_shapes=[pltpu.SemaphoreType.DMA((2, PAGES))],
    )(me_index.reshape(1), listing, page_table, cache)


def place_kernel(first_page, aliased, where_ref, source_ref, *refs):
    out_ref, held, load_sems, sems = refs[aliased:]
    slots, pages = held.shape[:2]

    def load(slot):
        return pltpu.make_async_copy(
            source_ref.at[where_ref[slot]], held.at[slot], load_sems.at[slot]
        )

    def store(slot):
        return pltpu.make_async_copy(
            held.at[slot], out_ref.at[slot, pl.ds(first_page, pages)], sems.at[slot]
        )

    @pl.loop(0, slots)
    def _(slot):
        load(slot).start()

    @pl.loop(0, slots)
    def _(slot):
        load(slot).wait()
        store(slot).start()

    @pl.loop(0, slots)
    def _(slot):
        store(slot).wait()


def place_children(where, source, first_page, earlier=None):
    slots = where.shape[0]
    given = [where, source] + ([] if earlier is None else [earlier])
    return pl.pallas_call(
        functools.partial(place_kernel, first_page, len(given) - 2),
        out_shape=jax.ShapeDtypeStruct((slots, PAGES) + source.shape[2:], source.dtype),
        in_specs=[
            pl.BlockSpec(memory_space=pltpu.SMEM),
            pl.BlockSpec(memory_space=pltpu.HBM),
        ]
        + [pl.BlockSpec(memory_space=pl.ANY)] * (len(given) - 2),
        out_specs=pl.BlockSpec(memory_space=pl.ANY),
        scratch_shapes=[
            pltpu.VMEM((slots,) + source.shape[1:], source.dtype),
            pltpu.SemaphoreType.DMA((slots,)),
            pltpu.SemaphoreType.DMA((slots,)),
        ],
        input_output_aliases={} if earlier is None else {2: 0},
        compiler_params=pltpu.CompilerParams(vmem_limit_bytes=58 * 2**20),
    )(*given)


def child_places(listing, fork_parent, me_index):
    owner = fork_parent // BR_DEV
    asked = listing.reshape(1, -1)
    same = (asked // BR_DEV) == owner[:, None]
    first = jnp.min(jnp.where(same, asked % BR_DEV, BR_DEV - 1), axis=1)
    which = (fork_parent % BR_DEV != first).astype(jnp.int32)
    owner_z, owner_y = owner // NY, owner % NY
    near = (me_index // NY - owner_z) % NEAR
    front = owner * 2 + which
    back = ((owner_y * NEAR + near) * (NZ // NEAR) + owner_z // NEAR) * 2 + which
    return front, back


def gather_fronts(front):
    width = front.shape[-1]
    plane = exchange(front.reshape(NY, -1, width), groups_y()).reshape(-1, width)
    fronts = lax.all_gather(plane, "dp", axis=0, tiled=True, axis_index_groups=groups_z())
    return fronts.reshape((-1,) + front.shape[2:])


def gather_backs_far(back):
    width = back.shape[-1]
    return exchange(back.reshape(NZ // NEAR, -1, width), groups_far()).reshape(-1, width)


def gather_backs_near(far):
    return jnp.concatenate(
        [far] + [lax.ppermute(far, "dp", shift_z(step)) for step in (1, 2, -1)]
    )


def halve(held, apart):
    shards = lax.axis_size("tensor")
    mine = (lax.axis_index("tensor") // apart) % 2
    pairs = held.reshape((-1, 2) + held.shape[1:])
    keep = lax.dynamic_index_in_dim(pairs, mine, 1, keepdims=False)
    send = lax.dynamic_index_in_dim(pairs, 1 - mine, 1, keepdims=False)
    came = lax.ppermute(send, "tensor", [(i, i ^ apart) for i in range(shards)])
    return keep.astype(jnp.float32) + came.astype(jnp.float32)


def local(
    queries,
    new_kv,
    kv_cache,
    page_table,
    lengths,
    out_proj,
    residual,
    norm_gain,
    score_weight,
    fork_parent,
):
    keys, values = cached(kv_cache, page_table)
    listing, queries, keys, values = lax.optimization_barrier(
        (parent_listing(fork_parent), queries, keys, values)
    )
    cache = kv_cache[:, :, :, 0]
    front, back = pick_pages(lax.axis_index("dp"), listing, page_table, cache)
    fronts = gather_fronts(front)
    attended = attend(queries, new_kv, keys, values, lengths)
    rows_here = residual.shape[0]
    partial = jnp.dot(attended, out_proj, preferred_element_type=jnp.float32).astype(jnp.bfloat16)
    far, partial = lax.optimization_barrier((gather_backs_far(back), partial))
    held = halve(partial.reshape(lax.axis_size("tensor"), rows_here, -1), 1).astype(jnp.bfloat16)
    column, held = lax.optimization_barrier((gather_backs_near(far), held))
    backs = share(column, groups_y()).reshape((-1,) + back.shape[2:])
    held = halve(held, 2).astype(jnp.bfloat16)
    updated = halve(held, 4)[0] + residual.astype(jnp.float32)
    hidden_out = updated.astype(jnp.bfloat16)
    block_ends = updated.reshape(rows_here // CH, CH, updated.shape[1])[:, CH - 1]
    normed = (
        block_ends
        * lax.rsqrt(jnp.mean(block_ends * block_ends, axis=-1, keepdims=True) + 1e-06)
        * norm_gain.astype(jnp.float32)
    )
    scores = jax.nn.sigmoid(jnp.sum(normed * score_weight.astype(jnp.float32), axis=-1))
    front_at, back_at = child_places(listing, fork_parent, lax.axis_index("dp"))
    child_pages = place_children(back_at, backs, FRONT)
    child_pages = place_children(front_at, fronts, 0, child_pages)[:, :, :, :, None]
    return (hidden_out, scores, child_pages)


def solution(mesh):
    in_specs = (
        P("dp", None, "tensor", None),
        P("dp", None, None, "tensor", None),
        P("dp", None, None, "tensor", None),
        P("dp", None),
        P("dp"),
        P("tensor", None),
        P(("dp", "tensor"), None),
        P(),
        P(),
        P("dp"),
    )
    out_specs = (
        P(("dp", "tensor"), None),
        P(("dp", "tensor")),
        P("dp", None, None, None, "tensor", None),
    )
    return jax.shard_map(local, mesh=mesh, in_specs=in_specs, out_specs=out_specs, check_vma=False)
```

```python
import functools

import jax
import jax.numpy as jnp
from jax import lax
from jax.experimental import pallas as pl
from jax.experimental.pallas import tpu as pltpu
from jax.sharding import PartitionSpec as P

BR_DEV = 16
CH = 16
PAGE = 16
PREFIX = 128
PAGES = PREFIX // PAGE
NZ, NY = 16, 4
NEAR = 4
FRONT = 6


neg_fill = -1e30

def cached(kv_cache, page_table):
    pages = kv_cache[page_table]
    branch, count, _, page, kvheads, head_width = pages.shape
    flat = (branch, count * page, kvheads, head_width)
    return pages[:, :, 0].reshape(flat), pages[:, :, 1].reshape(flat)


def attend(queries, new_kv, cache_keys, cache_values, lengths):
    branch, steps_new, qheads, head_width = queries.shape
    kvheads = new_kv.shape[3]
    per_group = qheads // kvheads
    key_span = cache_keys.shape[1]
    grouped = queries.reshape(branch, steps_new, kvheads, per_group, head_width)
    score_scale = head_width ** (-0.5)
    old_scores = (
        jnp.einsum("bckgd,bskd->bkgcs", grouped, cache_keys, preferred_element_type=jnp.float32)
        * score_scale
    )
    new_scores = (
        jnp.einsum("bckgd,btkd->bkgct", grouped, new_kv[:, 0], preferred_element_type=jnp.float32)
        * score_scale
    )
    old_mask = (jnp.arange(key_span)[None, :] < lengths[:, None])[:, None, None, None, :]
    new_mask = (jnp.arange(steps_new)[None, :] <= jnp.arange(steps_new)[:, None])[None, None, None]
    old_scores = jnp.where(old_mask, old_scores, neg_fill)
    new_scores = jnp.where(new_mask, new_scores, neg_fill)
    row_max = jnp.maximum(
        jnp.max(old_scores, axis=-1, keepdims=True), jnp.max(new_scores, axis=-1, keepdims=True)
    )
    old_probs = jnp.where(old_mask, jnp.exp(old_scores - row_max), 0.0)
    new_probs = jnp.where(new_mask, jnp.exp(new_scores - row_max), 0.0)
    denom_sum = jnp.sum(old_probs, axis=-1, keepdims=True) + jnp.sum(
        new_probs, axis=-1, keepdims=True
    )
    old_weights = (old_probs / denom_sum).astype(jnp.bfloat16)
    new_weights = (new_probs / denom_sum).astype(jnp.bfloat16)
    attended = jnp.einsum(
        "bkgcs,bskd->bckgd", old_weights, cache_values, preferred_element_type=jnp.float32
    )
    attended = attended + jnp.einsum(
        "bkgct,btkd->bckgd", new_weights, new_kv[:, 1], preferred_element_type=jnp.float32
    )
    return attended.astype(jnp.bfloat16).reshape(branch * steps_new, qheads * head_width)


def parent_listing(fork_parent):
    groups = lax.axis_size("dp")
    copies = jnp.broadcast_to(fork_parent[None, None, :], (groups, 1, fork_parent.shape[0]))
    return lax.all_to_all(copies, "dp", split_axis=0, concat_axis=0, tiled=True)[:, 0]


def shift_z(step):
    return [(z * NY + y, (z + step) % NZ * NY + y) for z in range(NZ) for y in range(NY)]


def groups_far():
    return [[(near + NEAR * far) * NY + y for far in range(NZ // NEAR)] for near in range(NEAR) for y in range(NY)]


def groups_z():
    return [[z * NY + y for z in range(NZ)] for y in range(NY)]


def groups_y():
    return [[z * NY + y for y in range(NY)] for z in range(NZ)]


def share(block, groups):
    return exchange(jnp.broadcast_to(block[None], (len(groups[0]),) + block.shape), groups)


def exchange(copies, groups):
    return lax.all_to_all(
        copies, "dp", split_axis=0, concat_axis=0, tiled=True, axis_index_groups=groups
    )


def pick_kernel(me_ref, listing_ref, table_ref, cache_ref, front_ref, back_ref, sems):
    asked = listing_ref[...]
    mine = (asked >> 4) == me_ref[0]
    rows = asked & (BR_DEV - 1)
    lowest = jnp.min(jnp.where(mine, rows, BR_DEV - 1))
    highest = jnp.max(jnp.where(mine, rows, 0))
    copies = []
    for which, row in enumerate((lowest, highest)):
        for page in range(PAGES):
            part, at = (front_ref, page) if page < FRONT else (back_ref, page - FRONT)
            copies.append(
                pltpu.make_async_copy(
                    cache_ref.at[table_ref[row, page]], part.at[0, which, at], sems.at[which, page]
                )
            )
    for copy in copies:
        copy.start()
    for copy in copies:
        copy.wait()
    for part in (front_ref, back_ref):
        for number in range(1, part.shape[0]):
            part[number] = part[0]


def pick_pages(me_index, listing, page_table, cache):
    return pl.pallas_call(
        pick_kernel,
        out_shape=tuple(
            jax.ShapeDtypeStruct((copies, 2, pages) + cache.shape[1:], cache.dtype)
            for copies, pages in ((NY, FRONT), (NZ // NEAR, PAGES - FRONT))
        ),
        in_specs=[
            pl.BlockSpec(memory_space=pltpu.SMEM),
            pl.BlockSpec(memory_space=pltpu.VMEM),
            pl.BlockSpec(memory_space=pltpu.SMEM),
            pl.BlockSpec(memory_space=pl.ANY),
        ],
        out_specs=(pl.BlockSpec(memory_space=pltpu.VMEM),) * 2,
        scratch_shapes=[pltpu.SemaphoreType.DMA((2, PAGES))],
    )(me_index.reshape(1), listing, page_table, cache)


def place_kernel(first_page, aliased, where_ref, source_ref, *refs):
    out_ref, held, load_sems, sems = refs[aliased:]
    slots, pages = held.shape[:2]

    def load(slot):
        return pltpu.make_async_copy(
            source_ref.at[where_ref[slot]], held.at[slot], load_sems.at[slot]
        )

    def store(slot):
        return pltpu.make_async_copy(
            held.at[slot], out_ref.at[slot, pl.ds(first_page, pages)], sems.at[slot]
        )

    for slot in range(slots):
        load(slot).start()
    for slot in range(slots):
        load(slot).wait()
        store(slot).start()
    for slot in range(slots):
        store(slot).wait()


def place_children(where, source, first_page, earlier=None):
    slots = where.shape[0]
    given = [where, source] + ([] if earlier is None else [earlier])
    return pl.pallas_call(
        functools.partial(place_kernel, first_page, len(given) - 2),
        out_shape=jax.ShapeDtypeStruct((slots, PAGES) + source.shape[2:], source.dtype),
        in_specs=[
            pl.BlockSpec(memory_space=pltpu.SMEM),
            pl.BlockSpec(memory_space=pltpu.HBM),
        ]
        + [pl.BlockSpec(memory_space=pl.ANY)] * (len(given) - 2),
        out_specs=pl.BlockSpec(memory_space=pl.ANY),
        scratch_shapes=[
            pltpu.VMEM((slots,) + source.shape[1:], source.dtype),
            pltpu.SemaphoreType.DMA((slots,)),
            pltpu.SemaphoreType.DMA((slots,)),
        ],
        input_output_aliases={} if earlier is None else {2: 0},
        compiler_params=pltpu.CompilerParams(vmem_limit_bytes=58 * 2**20),
    )(*given)


def child_places(listing, fork_parent, me_index):
    owner = fork_parent // BR_DEV
    asked = listing.reshape(1, -1)
    same = (asked // BR_DEV) == owner[:, None]
    first = jnp.min(jnp.where(same, asked % BR_DEV, BR_DEV - 1), axis=1)
    which = (fork_parent % BR_DEV != first).astype(jnp.int32)
    owner_z, owner_y = owner // NY, owner % NY
    near = (me_index // NY - owner_z) % NEAR
    front = owner * 2 + which
    back = ((owner_y * NEAR + near) * (NZ // NEAR) + owner_z // NEAR) * 2 + which
    return front, back


def gather_fronts(front):
    width = front.shape[-1]
    plane = exchange(front.reshape(NY, -1, width), groups_y()).reshape(-1, width)
    fronts = lax.all_gather(plane, "dp", axis=0, tiled=True, axis_index_groups=groups_z())
    return fronts.reshape((-1,) + front.shape[2:])


def gather_backs_far(back):
    width = back.shape[-1]
    return exchange(back.reshape(NZ // NEAR, -1, width), groups_far()).reshape(-1, width)


def gather_backs_near(far):
    return jnp.concatenate(
        [far] + [lax.ppermute(far, "dp", shift_z(step)) for step in (1, 2, -1)]
    )


def halve(held, apart):
    shards = lax.axis_size("tensor")
    mine = (lax.axis_index("tensor") // apart) % 2
    pairs = held.reshape((-1, 2) + held.shape[1:])
    keep = lax.dynamic_index_in_dim(pairs, mine, 1, keepdims=False)
    send = lax.dynamic_index_in_dim(pairs, 1 - mine, 1, keepdims=False)
    came = lax.ppermute(send, "tensor", [(i, i ^ apart) for i in range(shards)])
    return keep.astype(jnp.float32) + came.astype(jnp.float32)


def local(
    queries,
    new_kv,
    kv_cache,
    page_table,
    lengths,
    out_proj,
    residual,
    norm_gain,
    score_weight,
    fork_parent,
):
    keys, values = cached(kv_cache, page_table)
    listing, queries, keys, values = lax.optimization_barrier(
        (parent_listing(fork_parent), queries, keys, values)
    )
    cache = kv_cache[:, :, :, 0]
    front, back = pick_pages(lax.axis_index("dp"), listing, page_table, cache)
    fronts = gather_fronts(front)
    attended = attend(queries, new_kv, keys, values, lengths)
    rows_here = residual.shape[0]
    partial = jnp.dot(attended, out_proj, preferred_element_type=jnp.float32).astype(jnp.bfloat16)
    far, partial = lax.optimization_barrier((gather_backs_far(back), partial))
    held = halve(partial.reshape(lax.axis_size("tensor"), rows_here, -1), 1).astype(jnp.bfloat16)
    column, held = lax.optimization_barrier((gather_backs_near(far), held))
    backs = share(column, groups_y()).reshape((-1,) + back.shape[2:])
    held = halve(held, 2).astype(jnp.bfloat16)
    updated = halve(held, 4)[0] + residual.astype(jnp.float32)
    hidden_out = updated.astype(jnp.bfloat16)
    block_ends = updated.reshape(rows_here // CH, CH, updated.shape[1])[:, CH - 1]
    normed = (
        block_ends
        * lax.rsqrt(jnp.mean(block_ends * block_ends, axis=-1, keepdims=True) + 1e-06)
        * norm_gain.astype(jnp.float32)
    )
    scores = jax.nn.sigmoid(jnp.sum(normed * score_weight.astype(jnp.float32), axis=-1))
    front_at, back_at = child_places(listing, fork_parent, lax.axis_index("dp"))
    child_pages = place_children(back_at, backs, FRONT)
    child_pages = place_children(front_at, fronts, 0, child_pages)[:, :, :, :, None]
    return (hidden_out, scores, child_pages)


def solution(mesh):
    in_specs = (
        P("dp", None, "tensor", None),
        P("dp", None, None, "tensor", None),
        P("dp", None, None, "tensor", None),
        P("dp", None),
        P("dp"),
        P("tensor", None),
        P(("dp", "tensor"), None),
        P(),
        P(),
        P("dp"),
    )
    out_specs = (
        P(("dp", "tensor"), None),
        P(("dp", "tensor")),
        P("dp", None, None, None, "tensor", None),
    )
    return jax.shard_map(local, mesh=mesh, in_specs=in_specs, out_specs=out_specs, check_vma=False)
```

```python
import functools

import jax
import jax.numpy as jnp
from jax import lax
from jax.experimental import pallas as pl
from jax.experimental.pallas import tpu as pltpu
from jax.sharding import PartitionSpec as P

BR_DEV = 16
CH = 16
PAGE = 16
PREFIX = 128
PAGES = PREFIX // PAGE
NZ, NY = 16, 4
NEAR = 4
FRONT = 6
LANES = 128


neg_fill = -1e30

def cached(kv_cache, page_table):
    pages = kv_cache[page_table]
    branch, count, _, page, kvheads, head_width = pages.shape
    flat = (branch, count * page, kvheads, head_width)
    return pages[:, :, 0].reshape(flat), pages[:, :, 1].reshape(flat)


def attend(queries, new_kv, cache_keys, cache_values, lengths):
    branch, steps_new, qheads, head_width = queries.shape
    kvheads = new_kv.shape[3]
    per_group = qheads // kvheads
    key_span = cache_keys.shape[1]
    grouped = queries.reshape(branch, steps_new, kvheads, per_group, head_width)
    score_scale = head_width ** (-0.5)
    old_scores = (
        jnp.einsum("bckgd,bskd->bkgcs", grouped, cache_keys, preferred_element_type=jnp.float32)
        * score_scale
    )
    new_scores = (
        jnp.einsum("bckgd,btkd->bkgct", grouped, new_kv[:, 0], preferred_element_type=jnp.float32)
        * score_scale
    )
    old_mask = (jnp.arange(key_span)[None, :] < lengths[:, None])[:, None, None, None, :]
    new_mask = (jnp.arange(steps_new)[None, :] <= jnp.arange(steps_new)[:, None])[None, None, None]
    old_scores = jnp.where(old_mask, old_scores, neg_fill)
    new_scores = jnp.where(new_mask, new_scores, neg_fill)
    row_max = jnp.maximum(
        jnp.max(old_scores, axis=-1, keepdims=True), jnp.max(new_scores, axis=-1, keepdims=True)
    )
    old_probs = jnp.where(old_mask, jnp.exp(old_scores - row_max), 0.0)
    new_probs = jnp.where(new_mask, jnp.exp(new_scores - row_max), 0.0)
    denom_sum = jnp.sum(old_probs, axis=-1, keepdims=True) + jnp.sum(
        new_probs, axis=-1, keepdims=True
    )
    old_weights = (old_probs / denom_sum).astype(jnp.bfloat16)
    new_weights = (new_probs / denom_sum).astype(jnp.bfloat16)
    attended = jnp.einsum(
        "bkgcs,bskd->bckgd", old_weights, cache_values, preferred_element_type=jnp.float32
    )
    attended = attended + jnp.einsum(
        "bkgct,btkd->bckgd", new_weights, new_kv[:, 1], preferred_element_type=jnp.float32
    )
    return attended.astype(jnp.bfloat16).reshape(branch * steps_new, qheads * head_width)


def parent_listing(fork_parent):
    groups = lax.axis_size("dp")
    slots = fork_parent.shape[0]
    row = jnp.pad(fork_parent, (0, LANES - slots), constant_values=-1)
    copies = jnp.broadcast_to(row[None, None, :], (groups, 1, LANES))
    return lax.all_to_all(copies, "dp", split_axis=0, concat_axis=0, tiled=True)[:, 0]


def shift_z(step):
    return [(z * NY + y, (z + step) % NZ * NY + y) for z in range(NZ) for y in range(NY)]


def groups_far():
    return [[(near + NEAR * far) * NY + y for far in range(NZ // NEAR)] for near in range(NEAR) for y in range(NY)]


def groups_z():
    return [[z * NY + y for z in range(NZ)] for y in range(NY)]


def groups_y():
    return [[z * NY + y for y in range(NY)] for z in range(NZ)]


def share(block, groups):
    return exchange(jnp.broadcast_to(block[None], (len(groups[0]),) + block.shape), groups)


def exchange(copies, groups):
    return lax.all_to_all(
        copies, "dp", split_axis=0, concat_axis=0, tiled=True, axis_index_groups=groups
    )


def pick_kernel(me_ref, listing_ref, table_ref, cache_ref, front_ref, back_ref, sems):
    asked = listing_ref[...]
    mine = (asked >> 4) == me_ref[0]
    rows = asked & (BR_DEV - 1)
    lowest = jnp.min(jnp.where(mine, rows, BR_DEV - 1))
    highest = jnp.max(jnp.where(mine, rows, 0))
    copies = []
    for which, row in enumerate((lowest, highest)):
        for page in range(PAGES):
            part, at = (front_ref, page) if page < FRONT else (back_ref, page - FRONT)
            copies.append(
                pltpu.make_async_copy(
                    cache_ref.at[table_ref[row, page]], part.at[0, which, at], sems.at[which, page]
                )
            )
    for copy in copies:
        copy.start()
    for copy in copies:
        copy.wait()
    for part in (front_ref, back_ref):
        for number in range(1, part.shape[0]):
            part[number] = part[0]


def pick_pages(me_index, listing, page_table, cache):
    return pl.pallas_call(
        pick_kernel,
        out_shape=tuple(
            jax.ShapeDtypeStruct((copies, 2, pages) + cache.shape[1:], cache.dtype)
            for copies, pages in ((NY, FRONT), (NZ // NEAR, PAGES - FRONT))
        ),
        in_specs=[
            pl.BlockSpec(memory_space=pltpu.SMEM),
            pl.BlockSpec(memory_space=pltpu.VMEM),
            pl.BlockSpec(memory_space=pltpu.SMEM),
            pl.BlockSpec(memory_space=pl.ANY),
        ],
        out_specs=(pl.BlockSpec(memory_space=pltpu.VMEM),) * 2,
        scratch_shapes=[pltpu.SemaphoreType.DMA((2, PAGES))],
    )(me_index.reshape(1), listing, page_table, cache)


def place_kernel(first_page, aliased, where_ref, source_ref, *refs):
    out_ref, held, load_sems, sems = refs[aliased:]
    slots, pages = held.shape[:2]

    def load(slot):
        return pltpu.make_async_copy(
            source_ref.at[where_ref[slot]], held.at[slot], load_sems.at[slot]
        )

    def store(slot):
        return pltpu.make_async_copy(
            held.at[slot], out_ref.at[slot, pl.ds(first_page, pages)], sems.at[slot]
        )

    @pl.loop(0, slots)
    def _(slot):
        load(slot).start()

    @pl.loop(0, slots)
    def _(slot):
        load(slot).wait()
        store(slot).start()

    @pl.loop(0, slots)
    def _(slot):
        store(slot).wait()


def place_children(where, source, first_page, earlier=None):
    slots = where.shape[0]
    given = [where, source] + ([] if earlier is None else [earlier])
    return pl.pallas_call(
        functools.partial(place_kernel, first_page, len(given) - 2),
        out_shape=jax.ShapeDtypeStruct((slots, PAGES) + source.shape[2:], source.dtype),
        in_specs=[
            pl.BlockSpec(memory_space=pltpu.SMEM),
            pl.BlockSpec(memory_space=pltpu.HBM),
        ]
        + [pl.BlockSpec(memory_space=pl.ANY)] * (len(given) - 2),
        out_specs=pl.BlockSpec(memory_space=pl.ANY),
        scratch_shapes=[
            pltpu.VMEM((slots,) + source.shape[1:], source.dtype),
            pltpu.SemaphoreType.DMA((slots,)),
            pltpu.SemaphoreType.DMA((slots,)),
        ],
        input_output_aliases={} if earlier is None else {2: 0},
        compiler_params=pltpu.CompilerParams(vmem_limit_bytes=58 * 2**20),
    )(*given)


def child_places(listing, fork_parent, me_index):
    owner = fork_parent // BR_DEV
    asked = listing.reshape(1, -1)
    same = (asked // BR_DEV) == owner[:, None]
    first = jnp.min(jnp.where(same, asked % BR_DEV, BR_DEV - 1), axis=1)
    which = (fork_parent % BR_DEV != first).astype(jnp.int32)
    owner_z, owner_y = owner // NY, owner % NY
    near = (me_index // NY - owner_z) % NEAR
    front = owner * 2 + which
    back = ((owner_y * NEAR + near) * (NZ // NEAR) + owner_z // NEAR) * 2 + which
    return front, back


def gather_plane(front):
    return exchange(front.reshape(NY, -1, front.shape[-1]), groups_y())


def gather_fronts(plane, tile):
    plane = plane.reshape(-1, plane.shape[-1])
    fronts = lax.all_gather(plane, "dp", axis=0, tiled=True, axis_index_groups=groups_z())
    return fronts.reshape((-1,) + tile)


def gather_backs_far(back):
    width = back.shape[-1]
    return exchange(back.reshape(NZ // NEAR, -1, width), groups_far()).reshape(-1, width)


def gather_backs_near(far):
    half = far.shape[0] // 2
    sent = ((far, 1), (far[:half], 2), (far[half:], -2), (far, -1))
    return jnp.concatenate([far] + [lax.ppermute(x, "dp", shift_z(step)) for x, step in sent])


def halve(held, apart):
    shards = lax.axis_size("tensor")
    mine = (lax.axis_index("tensor") // apart) % 2
    pairs = held.reshape((-1, 2) + held.shape[1:])
    keep = lax.dynamic_index_in_dim(pairs, mine, 1, keepdims=False)
    send = lax.dynamic_index_in_dim(pairs, 1 - mine, 1, keepdims=False)
    came = lax.ppermute(send, "tensor", [(i, i ^ apart) for i in range(shards)])
    return keep.astype(jnp.float32) + came.astype(jnp.float32)


def local(
    queries,
    new_kv,
    kv_cache,
    page_table,
    lengths,
    out_proj,
    residual,
    norm_gain,
    score_weight,
    fork_parent,
):
    keys, values = cached(kv_cache, page_table)
    listing, keys, values = lax.optimization_barrier((parent_listing(fork_parent), keys, values))
    cache = kv_cache[:, :, :, 0]
    front, back = pick_pages(lax.axis_index("dp"), listing, page_table, cache)
    front, back, queries = lax.optimization_barrier((front, back, queries))
    attended = attend(queries, new_kv, keys, values, lengths)
    rows_here = residual.shape[0]
    partial = jnp.dot(attended, out_proj, preferred_element_type=jnp.float32).astype(jnp.bfloat16)
    plane, partial = lax.optimization_barrier((gather_plane(front), partial))
    fronts = gather_fronts(plane, front.shape[2:])
    held = partial.reshape(lax.axis_size("tensor"), rows_here, -1)
    held = halve(held, 1).astype(jnp.bfloat16)
    far, held = lax.optimization_barrier((gather_backs_far(back), held))
    held = halve(held, 2).astype(jnp.bfloat16)
    backs = share(gather_backs_near(far), groups_y()).reshape((-1,) + back.shape[2:])
    updated = halve(held, 4)[0] + residual.astype(jnp.float32)
    hidden_out = updated.astype(jnp.bfloat16)
    block_ends = updated.reshape(rows_here // CH, CH, updated.shape[1])[:, CH - 1]
    normed = (
        block_ends
        * lax.rsqrt(jnp.mean(block_ends * block_ends, axis=-1, keepdims=True) + 1e-06)
        * norm_gain.astype(jnp.float32)
    )
    scores = jax.nn.sigmoid(jnp.sum(normed * score_weight.astype(jnp.float32), axis=-1))
    front_at, back_at = child_places(listing, fork_parent, lax.axis_index("dp"))
    child_pages = place_children(back_at, backs, FRONT)
    child_pages = place_children(front_at, fronts, 0, child_pages)[:, :, :, :, None]
    return (hidden_out, scores, child_pages)


def solution(mesh):
    in_specs = (
        P("dp", None, "tensor", None),
        P("dp", None, None, "tensor", None),
        P("dp", None, None, "tensor", None),
        P("dp", None),
        P("dp"),
        P("tensor", None),
        P(("dp", "tensor"), None),
        P(),
        P(),
        P("dp"),
    )
    out_specs = (
        P(("dp", "tensor"), None),
        P(("dp", "tensor")),
        P("dp", None, None, None, "tensor", None),
    )
    return jax.shard_map(local, mesh=mesh, in_specs=in_specs, out_specs=out_specs, check_vma=False)
```

```python
import functools

import jax
import jax.numpy as jnp
from jax import lax
from jax.experimental import pallas as pl
from jax.experimental.pallas import tpu as pltpu
from jax.sharding import PartitionSpec as P

BR_DEV = 16
CH = 16
PAGE = 16
PREFIX = 128
PAGES = PREFIX // PAGE
NZ, NY = 16, 4
NEAR = 4
FRONT = (6, 5)
FRONT_AT = (0, FRONT[0])
BACK_AT = (0, PAGES - FRONT[0])
LANES = 128


neg_fill = -1e30

def cached(kv_cache, page_table):
    pages = kv_cache[page_table]
    branch, count, _, page, kvheads, head_width = pages.shape
    flat = (branch, count * page, kvheads, head_width)
    return pages[:, :, 0].reshape(flat), pages[:, :, 1].reshape(flat)


def attend(queries, new_kv, cache_keys, cache_values, lengths):
    branch, steps_new, qheads, head_width = queries.shape
    kvheads = new_kv.shape[3]
    per_group = qheads // kvheads
    key_span = cache_keys.shape[1]
    grouped = queries.reshape(branch, steps_new, kvheads, per_group, head_width)
    score_scale = head_width ** (-0.5)
    old_scores = (
        jnp.einsum("bckgd,bskd->bkgcs", grouped, cache_keys, preferred_element_type=jnp.float32)
        * score_scale
    )
    new_scores = (
        jnp.einsum("bckgd,btkd->bkgct", grouped, new_kv[:, 0], preferred_element_type=jnp.float32)
        * score_scale
    )
    old_mask = (jnp.arange(key_span)[None, :] < lengths[:, None])[:, None, None, None, :]
    new_mask = (jnp.arange(steps_new)[None, :] <= jnp.arange(steps_new)[:, None])[None, None, None]
    old_scores = jnp.where(old_mask, old_scores, neg_fill)
    new_scores = jnp.where(new_mask, new_scores, neg_fill)
    row_max = jnp.maximum(
        jnp.max(old_scores, axis=-1, keepdims=True), jnp.max(new_scores, axis=-1, keepdims=True)
    )
    old_probs = jnp.where(old_mask, jnp.exp(old_scores - row_max), 0.0)
    new_probs = jnp.where(new_mask, jnp.exp(new_scores - row_max), 0.0)
    denom_sum = jnp.sum(old_probs, axis=-1, keepdims=True) + jnp.sum(
        new_probs, axis=-1, keepdims=True
    )
    old_weights = (old_probs / denom_sum).astype(jnp.bfloat16)
    new_weights = (new_probs / denom_sum).astype(jnp.bfloat16)
    attended = jnp.einsum(
        "bkgcs,bskd->bckgd", old_weights, cache_values, preferred_element_type=jnp.float32
    )
    attended = attended + jnp.einsum(
        "bkgct,btkd->bckgd", new_weights, new_kv[:, 1], preferred_element_type=jnp.float32
    )
    return attended.astype(jnp.bfloat16).reshape(branch * steps_new, qheads * head_width)


def parent_listing(fork_parent):
    groups = lax.axis_size("dp")
    slots = fork_parent.shape[0]
    row = jnp.pad(fork_parent, (0, LANES - slots), constant_values=-1)
    copies = jnp.broadcast_to(row[None, None, :], (groups, 1, LANES))
    return lax.all_to_all(copies, "dp", split_axis=0, concat_axis=0, tiled=True)[:, 0]


def shift_z(step):
    return [(z * NY + y, (z + step) % NZ * NY + y) for z in range(NZ) for y in range(NY)]


def groups_far():
    return [[(near + NEAR * far) * NY + y for far in range(NZ // NEAR)] for near in range(NEAR) for y in range(NY)]


def groups_z():
    return [[z * NY + y for z in range(NZ)] for y in range(NY)]


def groups_y():
    return [[z * NY + y for y in range(NY)] for z in range(NZ)]


def share(block, groups):
    return exchange(jnp.broadcast_to(block[None], (len(groups[0]),) + block.shape), groups)


def exchange(copies, groups):
    return lax.all_to_all(
        copies, "dp", split_axis=0, concat_axis=0, tiled=True, axis_index_groups=groups
    )


def pick_kernel(me_ref, listing_ref, table_ref, cache_ref, front_ref, back_ref, sems):
    asked = listing_ref[...]
    mine = (asked >> 4) == me_ref[0]
    rows = asked & (BR_DEV - 1)
    lowest = jnp.min(jnp.where(mine, rows, BR_DEV - 1))
    highest = jnp.max(jnp.where(mine, rows, 0))
    copies = []
    for which, row in enumerate((lowest, highest)):
        for page in range(PAGES):
            if page < FRONT[which]:
                target = front_ref.at[0, FRONT_AT[which] + page]
            else:
                target = back_ref.at[0, BACK_AT[which] + page - FRONT[which]]
            copies.append(
                pltpu.make_async_copy(
                    cache_ref.at[table_ref[row, page]], target, sems.at[which, page]
                )
            )
    for copy in copies:
        copy.start()
    for copy in copies:
        copy.wait()
    for part in (front_ref, back_ref):
        for number in range(1, part.shape[0]):
            part[number] = part[0]


def pick_pages(me_index, listing, page_table, cache):
    return pl.pallas_call(
        pick_kernel,
        out_shape=tuple(
            jax.ShapeDtypeStruct((copies, pages) + cache.shape[1:], cache.dtype)
            for copies, pages in ((NY, sum(FRONT)), (NZ // NEAR, 2 * PAGES - sum(FRONT)))
        ),
        in_specs=[
            pl.BlockSpec(memory_space=pltpu.SMEM),
            pl.BlockSpec(memory_space=pltpu.VMEM),
            pl.BlockSpec(memory_space=pltpu.SMEM),
            pl.BlockSpec(memory_space=pl.ANY),
        ],
        out_specs=(pl.BlockSpec(memory_space=pltpu.VMEM),) * 2,
        scratch_shapes=[pltpu.SemaphoreType.DMA((2, PAGES))],
    )(me_index.reshape(1), listing, page_table, cache)


def place_kernel(spans, aliased, where_ref, source_ref, *refs):
    out_ref, held, load_sems, sems = refs[aliased:]
    slots = held.shape[0]

    def load(slot, span):
        first, pages, _ = span
        block = source_ref.at[where_ref[slot] >> 1, pl.ds(first, pages)]
        return pltpu.make_async_copy(block, held.at[slot, pl.ds(0, pages)], load_sems.at[slot])

    def store(slot, span):
        _, pages, target = span
        return pltpu.make_async_copy(
            held.at[slot, pl.ds(0, pages)], out_ref.at[slot, pl.ds(target, pages)], sems.at[slot]
        )

    def each_slot(step):
        @pl.loop(0, slots)
        def _(slot):
            for which, span in enumerate(spans):

                @pl.when((where_ref[slot] & 1) == which)
                def _():
                    step(slot, span)

    def pass_on(slot, span):
        load(slot, span).wait()
        store(slot, span).start()

    each_slot(lambda slot, span: load(slot, span).start())
    each_slot(pass_on)
    each_slot(lambda slot, span: store(slot, span).wait())


def place_children(where, source, spans, earlier=None):
    slots = where.shape[0]
    given = [where, source] + ([] if earlier is None else [earlier])
    return pl.pallas_call(
        functools.partial(place_kernel, spans, len(given) - 2),
        out_shape=jax.ShapeDtypeStruct((slots, PAGES) + source.shape[2:], source.dtype),
        in_specs=[
            pl.BlockSpec(memory_space=pltpu.SMEM),
            pl.BlockSpec(memory_space=pltpu.HBM),
        ]
        + [pl.BlockSpec(memory_space=pl.ANY)] * (len(given) - 2),
        out_specs=pl.BlockSpec(memory_space=pl.ANY),
        scratch_shapes=[
            pltpu.VMEM((slots, max(span[1] for span in spans)) + source.shape[2:], source.dtype),
            pltpu.SemaphoreType.DMA((slots,)),
            pltpu.SemaphoreType.DMA((slots,)),
        ],
        input_output_aliases={} if earlier is None else {2: 0},
        compiler_params=pltpu.CompilerParams(vmem_limit_bytes=58 * 2**20),
    )(*given)


def child_places(listing, fork_parent, me_index):
    owner = fork_parent // BR_DEV
    asked = listing.reshape(1, -1)
    same = (asked // BR_DEV) == owner[:, None]
    first = jnp.min(jnp.where(same, asked % BR_DEV, BR_DEV - 1), axis=1)
    which = (fork_parent % BR_DEV != first).astype(jnp.int32)
    owner_z, owner_y = owner // NY, owner % NY
    near = (me_index // NY - owner_z) % NEAR
    front = owner * 2 + which
    back = ((owner_y * NEAR + near) * (NZ // NEAR) + owner_z // NEAR) * 2 + which
    return front, back


def gather_plane(front):
    return exchange(front.reshape(NY, -1, front.shape[-1]), groups_y())


def gather_fronts(plane, tile):
    plane = plane.reshape(-1, plane.shape[-1])
    fronts = lax.all_gather(plane, "dp", axis=0, tiled=True, axis_index_groups=groups_z())
    return fronts.reshape((-1,) + tile)


def gather_backs_far(back):
    width = back.shape[-1]
    return exchange(back.reshape(NZ // NEAR, -1, width), groups_far()).reshape(-1, width)


def gather_backs_near(far):
    half = far.shape[0] // 2
    sent = ((far, 1), (far[:half], 2), (far[half:], -2), (far, -1))
    return jnp.concatenate([far] + [lax.ppermute(x, "dp", shift_z(step)) for x, step in sent])


def halve(held, apart):
    shards = lax.axis_size("tensor")
    mine = (lax.axis_index("tensor") // apart) % 2
    pairs = held.reshape((-1, 2) + held.shape[1:])
    keep = lax.dynamic_index_in_dim(pairs, mine, 1, keepdims=False)
    send = lax.dynamic_index_in_dim(pairs, 1 - mine, 1, keepdims=False)
    came = lax.ppermute(send, "tensor", [(i, i ^ apart) for i in range(shards)])
    return keep.astype(jnp.float32) + came.astype(jnp.float32)


def local(
    queries,
    new_kv,
    kv_cache,
    page_table,
    lengths,
    out_proj,
    residual,
    norm_gain,
    score_weight,
    fork_parent,
):
    keys, values = cached(kv_cache, page_table)
    listing, keys, values = lax.optimization_barrier((parent_listing(fork_parent), keys, values))
    cache = kv_cache[:, :, :, 0]
    front, back = pick_pages(lax.axis_index("dp"), listing, page_table, cache)
    front, back, queries = lax.optimization_barrier((front, back, queries))
    attended = attend(queries, new_kv, keys, values, lengths)
    rows_here = residual.shape[0]
    partial = jnp.dot(attended, out_proj, preferred_element_type=jnp.float32).astype(jnp.bfloat16)
    plane, partial = lax.optimization_barrier((gather_plane(front), partial))
    fronts = gather_fronts(plane, front.shape[1:])
    held = partial.reshape(lax.axis_size("tensor"), rows_here, -1)
    held = halve(held, 1).astype(jnp.bfloat16)
    far, held = lax.optimization_barrier((gather_backs_far(back), held))
    held = halve(held, 2).astype(jnp.bfloat16)
    backs = share(gather_backs_near(far), groups_y()).reshape((-1,) + back.shape[1:])
    updated = halve(held, 4)[0] + residual.astype(jnp.float32)
    hidden_out = updated.astype(jnp.bfloat16)
    block_ends = updated.reshape(rows_here // CH, CH, updated.shape[1])[:, CH - 1]
    normed = (
        block_ends
        * lax.rsqrt(jnp.mean(block_ends * block_ends, axis=-1, keepdims=True) + 1e-06)
        * norm_gain.astype(jnp.float32)
    )
    scores = jax.nn.sigmoid(jnp.sum(normed * score_weight.astype(jnp.float32), axis=-1))
    front_at, back_at = child_places(listing, fork_parent, lax.axis_index("dp"))
    front_spans = [(FRONT_AT[which], FRONT[which], 0) for which in range(2)]
    back_spans = [(BACK_AT[which], PAGES - FRONT[which], FRONT[which]) for which in range(2)]
    child_pages = place_children(back_at, backs, back_spans)
    child_pages = place_children(front_at, fronts, front_spans, child_pages)[:, :, :, :, None]
    return (hidden_out, scores, child_pages)


def solution(mesh):
    in_specs = (
        P("dp", None, "tensor", None),
        P("dp", None, None, "tensor", None),
        P("dp", None, None, "tensor", None),
        P("dp", None),
        P("dp"),
        P("tensor", None),
        P(("dp", "tensor"), None),
        P(),
        P(),
        P("dp"),
    )
    out_specs = (
        P(("dp", "tensor"), None),
        P(("dp", "tensor")),
        P("dp", None, None, None, "tensor", None),
    )
    return jax.shard_map(local, mesh=mesh, in_specs=in_specs, out_specs=out_specs, check_vma=False)
```

```python
import functools

import jax
import jax.numpy as jnp
from jax import lax
from jax.experimental import pallas as pl
from jax.experimental.pallas import tpu as pltpu
from jax.sharding import PartitionSpec as P

BR_DEV = 16
CH = 16
PAGE = 16
PREFIX = 128
PAGES = PREFIX // PAGE
NZ, NY = 16, 4
NEAR = 4
FRONT = 6
LANES = 128


neg_fill = -1e30

def cached(kv_cache, page_table):
    pages = kv_cache[page_table]
    branch, count, _, page, kvheads, head_width = pages.shape
    flat = (branch, count * page, kvheads, head_width)
    return pages[:, :, 0].reshape(flat), pages[:, :, 1].reshape(flat)


def attend(queries, new_kv, cache_keys, cache_values, lengths):
    branch, steps_new, qheads, head_width = queries.shape
    kvheads = new_kv.shape[3]
    per_group = qheads // kvheads
    key_span = cache_keys.shape[1]
    grouped = queries.reshape(branch, steps_new, kvheads, per_group, head_width)
    score_scale = head_width ** (-0.5)
    old_scores = (
        jnp.einsum("bckgd,bskd->bkgcs", grouped, cache_keys, preferred_element_type=jnp.float32)
        * score_scale
    )
    new_scores = (
        jnp.einsum("bckgd,btkd->bkgct", grouped, new_kv[:, 0], preferred_element_type=jnp.float32)
        * score_scale
    )
    old_mask = (jnp.arange(key_span)[None, :] < lengths[:, None])[:, None, None, None, :]
    new_mask = (jnp.arange(steps_new)[None, :] <= jnp.arange(steps_new)[:, None])[None, None, None]
    old_scores = jnp.where(old_mask, old_scores, neg_fill)
    new_scores = jnp.where(new_mask, new_scores, neg_fill)
    row_max = jnp.maximum(
        jnp.max(old_scores, axis=-1, keepdims=True), jnp.max(new_scores, axis=-1, keepdims=True)
    )
    old_probs = jnp.where(old_mask, jnp.exp(old_scores - row_max), 0.0)
    new_probs = jnp.where(new_mask, jnp.exp(new_scores - row_max), 0.0)
    denom_sum = jnp.sum(old_probs, axis=-1, keepdims=True) + jnp.sum(
        new_probs, axis=-1, keepdims=True
    )
    old_weights = (old_probs / denom_sum).astype(jnp.bfloat16)
    new_weights = (new_probs / denom_sum).astype(jnp.bfloat16)
    attended = jnp.einsum(
        "bkgcs,bskd->bckgd", old_weights, cache_values, preferred_element_type=jnp.float32
    )
    attended = attended + jnp.einsum(
        "bkgct,btkd->bckgd", new_weights, new_kv[:, 1], preferred_element_type=jnp.float32
    )
    return attended.astype(jnp.bfloat16).reshape(branch * steps_new, qheads * head_width)


def parent_listing(fork_parent):
    groups = lax.axis_size("dp")
    slots = fork_parent.shape[0]
    row = jnp.pad(fork_parent, (0, LANES - slots), constant_values=-1)
    copies = jnp.broadcast_to(row[None, None, :], (groups, 1, LANES))
    return lax.all_to_all(copies, "dp", split_axis=0, concat_axis=0, tiled=True)[:, 0]


def shift_z(step):
    return [(z * NY + y, (z + step) % NZ * NY + y) for z in range(NZ) for y in range(NY)]


def groups_far():
    return [[(near + NEAR * far) * NY + y for far in range(NZ // NEAR)] for near in range(NEAR) for y in range(NY)]


def groups_z():
    return [[z * NY + y for z in range(NZ)] for y in range(NY)]


def groups_y():
    return [[z * NY + y for y in range(NY)] for z in range(NZ)]


def share(block, groups):
    return exchange(jnp.broadcast_to(block[None], (len(groups[0]),) + block.shape), groups)


def exchange(copies, groups):
    return lax.all_to_all(
        copies, "dp", split_axis=0, concat_axis=0, tiled=True, axis_index_groups=groups
    )


def pick_kernel(me_ref, listing_ref, table_ref, cache_ref, front_ref, back_ref):
    asked = listing_ref[...]
    mine = (asked >> 4) == me_ref[0]
    rows = asked & (BR_DEV - 1)
    lowest = jnp.min(jnp.where(mine, rows, BR_DEV - 1))
    highest = jnp.max(jnp.where(mine, rows, 0))
    for which, row in enumerate((lowest, highest)):
        for page in range(PAGES):
            part, at = (front_ref, page) if page < FRONT else (back_ref, page - FRONT)
            block = cache_ref[table_ref[row, page]]
            for number in range(part.shape[0]):
                part[number, which, at] = block


def pick_pages(me_index, listing, page_table, cache):
    return pl.pallas_call(
        pick_kernel,
        out_shape=tuple(
            jax.ShapeDtypeStruct((copies, 2, pages) + cache.shape[1:], cache.dtype)
            for copies, pages in ((NY, FRONT), (NZ // NEAR, PAGES - FRONT))
        ),
        in_specs=[
            pl.BlockSpec(memory_space=pltpu.SMEM),
            pl.BlockSpec(memory_space=pltpu.VMEM),
            pl.BlockSpec(memory_space=pltpu.SMEM),
            pl.BlockSpec(memory_space=pltpu.VMEM),
        ],
        out_specs=(pl.BlockSpec(memory_space=pltpu.VMEM),) * 2,
        compiler_params=pltpu.CompilerParams(vmem_limit_bytes=16 * 2**20),
    )(me_index.reshape(1), listing, page_table, cache)


def place_kernel(first_page, aliased, where_ref, source_ref, *refs):
    out_ref, held, load_sems, sems = refs[aliased:]
    slots, pages = held.shape[:2]

    def load(slot):
        return pltpu.make_async_copy(
            source_ref.at[where_ref[slot]], held.at[slot], load_sems.at[slot]
        )

    def store(slot):
        return pltpu.make_async_copy(
            held.at[slot], out_ref.at[slot, pl.ds(first_page, pages)], sems.at[slot]
        )

    @pl.loop(0, slots)
    def _(slot):
        load(slot).start()

    @pl.loop(0, slots)
    def _(slot):
        load(slot).wait()
        store(slot).start()

    @pl.loop(0, slots)
    def _(slot):
        store(slot).wait()


def place_children(where, source, first_page, earlier=None):
    slots = where.shape[0]
    given = [where, source] + ([] if earlier is None else [earlier])
    return pl.pallas_call(
        functools.partial(place_kernel, first_page, len(given) - 2),
        out_shape=jax.ShapeDtypeStruct((slots, PAGES) + source.shape[2:], source.dtype),
        in_specs=[
            pl.BlockSpec(memory_space=pltpu.SMEM),
            pl.BlockSpec(memory_space=pltpu.HBM),
        ]
        + [pl.BlockSpec(memory_space=pl.ANY)] * (len(given) - 2),
        out_specs=pl.BlockSpec(memory_space=pl.ANY),
        scratch_shapes=[
            pltpu.VMEM((slots,) + source.shape[1:], source.dtype),
            pltpu.SemaphoreType.DMA((slots,)),
            pltpu.SemaphoreType.DMA((slots,)),
        ],
        input_output_aliases={} if earlier is None else {2: 0},
        compiler_params=pltpu.CompilerParams(vmem_limit_bytes=58 * 2**20),
    )(*given)


def child_places(listing, fork_parent, me_index):
    owner = fork_parent // BR_DEV
    asked = listing.reshape(1, -1)
    same = (asked // BR_DEV) == owner[:, None]
    first = jnp.min(jnp.where(same, asked % BR_DEV, BR_DEV - 1), axis=1)
    which = (fork_parent % BR_DEV != first).astype(jnp.int32)
    owner_z, owner_y = owner // NY, owner % NY
    near = (me_index // NY - owner_z) % NEAR
    front = owner * 2 + which
    back = ((owner_y * NEAR + near) * (NZ // NEAR) + owner_z // NEAR) * 2 + which
    return front, back


def gather_fronts(front):
    width = front.shape[-1]
    plane = exchange(front.reshape(NY, -1, width), groups_y()).reshape(-1, width)
    fronts = lax.all_gather(plane, "dp", axis=0, tiled=True, axis_index_groups=groups_z())
    return fronts.reshape((-1,) + front.shape[2:])


def gather_backs_far(back):
    width = back.shape[-1]
    return exchange(back.reshape(NZ // NEAR, -1, width), groups_far()).reshape(-1, width)


def gather_backs_near(far):
    return jnp.concatenate(
        [far] + [lax.ppermute(far, "dp", shift_z(step)) for step in (1, 2, -1)]
    )


def halve(held, apart):
    shards = lax.axis_size("tensor")
    mine = (lax.axis_index("tensor") // apart) % 2
    pairs = held.reshape((-1, 2) + held.shape[1:])
    keep = lax.dynamic_index_in_dim(pairs, mine, 1, keepdims=False)
    send = lax.dynamic_index_in_dim(pairs, 1 - mine, 1, keepdims=False)
    came = lax.ppermute(send, "tensor", [(i, i ^ apart) for i in range(shards)])
    return keep.astype(jnp.float32) + came.astype(jnp.float32)


def local(
    queries,
    new_kv,
    kv_cache,
    page_table,
    lengths,
    out_proj,
    residual,
    norm_gain,
    score_weight,
    fork_parent,
):
    keys, values = cached(kv_cache, page_table)
    listing, queries, keys, values = lax.optimization_barrier(
        (parent_listing(fork_parent), queries, keys, values)
    )
    cache = kv_cache[:, :, :, 0]
    front, back = pick_pages(lax.axis_index("dp"), listing, page_table, cache)
    fronts = gather_fronts(front)
    attended = attend(queries, new_kv, keys, values, lengths)
    rows_here = residual.shape[0]
    partial = jnp.dot(attended, out_proj, preferred_element_type=jnp.float32).astype(jnp.bfloat16)
    far, partial = lax.optimization_barrier((gather_backs_far(back), partial))
    held = halve(partial.reshape(lax.axis_size("tensor"), rows_here, -1), 1).astype(jnp.bfloat16)
    column, held = lax.optimization_barrier((gather_backs_near(far), held))
    backs = share(column, groups_y()).reshape((-1,) + back.shape[2:])
    held = halve(held, 2).astype(jnp.bfloat16)
    updated = halve(held, 4)[0] + residual.astype(jnp.float32)
    hidden_out = updated.astype(jnp.bfloat16)
    block_ends = updated.reshape(rows_here // CH, CH, updated.shape[1])[:, CH - 1]
    normed = (
        block_ends
        * lax.rsqrt(jnp.mean(block_ends * block_ends, axis=-1, keepdims=True) + 1e-06)
        * norm_gain.astype(jnp.float32)
    )
    scores = jax.nn.sigmoid(jnp.sum(normed * score_weight.astype(jnp.float32), axis=-1))
    front_at, back_at = child_places(listing, fork_parent, lax.axis_index("dp"))
    child_pages = place_children(back_at, backs, FRONT)
    child_pages = place_children(front_at, fronts, 0, child_pages)[:, :, :, :, None]
    return (hidden_out, scores, child_pages)


def solution(mesh):
    in_specs = (
        P("dp", None, "tensor", None),
        P("dp", None, None, "tensor", None),
        P("dp", None, None, "tensor", None),
        P("dp", None),
        P("dp"),
        P("tensor", None),
        P(("dp", "tensor"), None),
        P(),
        P(),
        P("dp"),
    )
    out_specs = (
        P(("dp", "tensor"), None),
        P(("dp", "tensor")),
        P("dp", None, None, None, "tensor", None),
    )
    return jax.shard_map(local, mesh=mesh, in_specs=in_specs, out_specs=out_specs, check_vma=False)
```
